32 devices in a mesh: expert: 8 (over z, y), dp: 4 (over x, core).
Axes of the slice: x: 2, y: 2, z: 4, core: 2. Of those that a mesh axis runs over, the one named last changes fastest.
Arguments:
- grads: bfloat16 [4, 16, 128, 1536], P('dp', 'expert'), may hold values from -6 to 6
- master: float32 [8, 128, 1536], P('expert', 'dp'), may hold values from -0.12 to 0.12
- moment: float32 [8, 128, 1536], P('expert', 'dp'), may hold values from -0.4 to 0.4
- second: float32 [8, 128, 1536], P('expert', 'dp'), may hold values from 0.001 to 0.01
- old_place: int32 [8, 2], replicated, may hold values from 0 to 7, all different within a row
- new_place: int32 [8, 2], replicated, may hold values from 0 to 7, all different within a row
- owner_slot: int32 [8], replicated, may hold values from 0 to 7, as said below
Outputs:
- new_master: float32 [8, 128, 1536], P('expert', 'dp')
- new_moment: float32 [8, 128, 1536], P('expert', 'dp')
- new_second: float32 [8, 128, 1536], P('expert', 'dp')
- replicas: bfloat16 [16, 128, 1536], P('expert', 'dp')
The draws below stay inside these ranges and needn't reach their ends.
Inputs may be any that keep to these rules, and one draw needn't show every extreme that they name: `owner_slot`: distinct values; the expert's owner is device value // 1 of the expert axis, in its owner slot value % 1. Slots that no expert names hold unused state. `old_place`: each device's 2 slots name distinct experts; every expert is named by some slot. `new_place`: each device's 2 slots name distinct experts; every expert is named by some slot.
All inputs are finite; a program needn't handle non-finite values.
Results may differ from the reference program's by a relative error of at most 0.015.
Values may be sent and summed in bfloat16 or wider, within the bound.
A program may use at most 64 MiB of HBM per device.

```python
import math
import jax
import jax.numpy as jnp
from jax import lax

H = 1536
ROWS = 128
EXPERTS = 8
OWN_MAX = 1
REP = 2
N_EXPERT = 8
N_DP = 4


def draw_owner_slot(key, part):
    key = jax.random.fold_in(key, 7)
    slot_total = N_EXPERT * OWN_MAX
    key_first, key_second = jax.random.split(key)
    middle_slots = jax.random.permutation(key_first, slot_total - 2)[:EXPERTS - 2] + 1
    chosen_slots = jnp.concatenate([jnp.array([0, slot_total - 1], jnp.int32), middle_slots.astype(jnp.int32)])
    return jax.random.permutation(key_second, chosen_slots).astype(jnp.int32)


def steps_of(rng, shape, cuts, smallest, high):
    gain, own = 1.0, jax.random.fold_in(rng, 6)
    for axis_at, shards_of in cuts:
        draws = jnp.exp(jax.random.uniform(jax.random.fold_in(own, axis_at), (shards_of,), jnp.float32, smallest / len(cuts), high / len(cuts)))
        gain = gain * jnp.repeat(draws, shape[axis_at] // shards_of).reshape([-1 if axis == axis_at else 1 for axis in range(len(shape))])
    return gain


def choose_distinct(rng, rows, amount, top, lift):
    order = jax.random.permutation(jax.random.fold_in(rng, 1), amount)
    pull = order
    for power in range(3):
        pull = pull * pull // amount
    pull = pull * lift // amount
    lots = jax.random.randint(jax.random.fold_in(rng, 2), (rows, amount), 0, 4096) + pull
    fixed_rows = jax.random.permutation(jax.random.fold_in(rng, 3), rows)[jnp.arange(amount) % rows]
    lots = jnp.where(jnp.arange(rows)[:, None] == fixed_rows[None, :], 1 << 14, lots)
    priority = lots * amount + jnp.arange(amount)
    return lax.top_k(priority.astype(jnp.int32), top)[1].astype(jnp.int32)


def bell_draw(key, shape, scale, most, pieces=(), dtype=jnp.bfloat16):
    entries = jax.random.normal(key, shape, jnp.float32) * scale
    if len(pieces) > 0:
        entries = steps_of(key, shape, pieces, -0.22, 0.18) * entries
    return jnp.clip(entries, min=-most, max=most).astype(dtype)


def setup_inputs(seed: int = 0) -> dict:
    splits = jax.random.split(jax.random.key(seed), 8)
    grads = bell_draw(splits[0], (N_DP, N_EXPERT * REP, ROWS, H), 1.0, 6.0, ((0, 4), (1, 8)))
    master = bell_draw(splits[1], (N_EXPERT * OWN_MAX, ROWS, H), 0.03, 0.12, ((0, 8), (1, 4)), jnp.float32)
    moment = bell_draw(splits[2], (N_EXPERT * OWN_MAX, ROWS, H), 0.1, 0.4, ((0, 8), (1, 4)), jnp.float32)
    second = jnp.clip(jnp.exp(math.log(0.01) - 2.30258502 * jax.random.uniform(splits[3], (N_EXPERT * OWN_MAX, ROWS, H), jnp.float32) ** steps_of(splits[3], (N_EXPERT * OWN_MAX, ROWS, H), ((0, 8), (1, 4)), -0.2, 0.2)), 0.001, 0.01)
    old_place = choose_distinct(splits[4], N_EXPERT, EXPERTS, REP, 4096)
    new_place = choose_distinct(splits[5], N_EXPERT, EXPERTS, REP, 4096)
    owner_slot = draw_owner_slot(jax.random.fold_in(splits[7], 71), 0)
    return {"grads": grads, "master": master, "moment": moment, "second": second, "old_place": old_place, "new_place": new_place, "owner_slot": owner_slot}


beta_first = 0.9
beta_second = 0.999
learn_rate = 0.02
weight_decay = 0.1
epsilon = 1e-08
scale_first = 1.0 - 0.9 ** 40
scale_second = 1.0 - 0.999 ** 40

def reference(grads, master, moment, second, old_place, new_place, owner_slot):
    flat_old = old_place.reshape(-1).astype(jnp.int32)
    expert_grad = jnp.zeros((EXPERTS, ROWS, H), jnp.float32)
    for member in range(N_DP):
        expert_grad = expert_grad + jax.ops.segment_sum(grads[member].astype(jnp.float32), flat_old, num_segments=EXPERTS)
    slot_grad = jnp.zeros(master.shape, jnp.float32).at[owner_slot.astype(jnp.int32)].set(expert_grad)
    new_moment = beta_first * moment + (1.0 - beta_first) * slot_grad
    new_second = beta_second * second + (1.0 - beta_second) * slot_grad * slot_grad
    update = new_moment / scale_first / (jnp.sqrt(new_second / scale_second) + epsilon)
    new_master = master - learn_rate * (update + weight_decay * master)
    chosen = owner_slot[new_place.reshape(-1).astype(jnp.int32)].astype(jnp.int32)
    replicas = new_master[chosen].astype(jnp.bfloat16)
    return (new_master, new_moment, new_second, replicas)
```

```python
import functools

import jax
import jax.numpy as jnp
from jax import lax
from jax.experimental import pallas as pl
from jax.experimental.pallas import tpu as pltpu
from jax.sharding import PartitionSpec as P

beta_first = 0.9
beta_second = 0.999
learn_rate = 0.02
weight_decay = 0.1
epsilon = 1e-08
scale_first = 1.0 - 0.9**40
scale_second = 1.0 - 0.999**40
MESH = pl.DeviceIdType.MESH
F32 = jnp.float32
BF16 = jnp.bfloat16
TILE = 16


def adam(master, moment, second, grad):
    new_moment = beta_first * moment + (1.0 - beta_first) * grad
    new_second = beta_second * second + (1.0 - beta_second) * grad * grad
    update = new_moment / scale_first / (jnp.sqrt(new_second / scale_second) + epsilon)
    new_master = master - learn_rate * (update + weight_decay * master)
    return new_master, new_moment, new_second


def piece_at(j, width):
    rows = pl.ds(pl.multiple_of(((j // 2) % 2) * TILE, TILE), TILE)
    cols = pl.ds(pl.multiple_of(((j // 4) * 2 + j % 2) * width, 128), width)
    return rows, cols


def kernel(
    n,
    grads,
    master,
    moment,
    second,
    old_place,
    new_place,
    owner_slot,
    slot_grad,
    replicas,
    own,
    core_in,
    cross_out,
    cross_in,
    summed,
    incoming,
    acc,
    to_owner,
    state,
    state_out,
    pieces_in,
    fresh,
    outbound,
    load_sem,
    core_sem,
    cross_sem,
    part_send,
    part_recv,
    state_send,
    state_recv,
    owner_send,
    owner_recv,
    fresh_send,
    fresh_recv,
):
    me = lax.axis_index("expert")
    dp = lax.axis_index("dp")
    x, core = dp // 2, dp % 2
    near = x * 2 + (1 - core)
    far = (1 - x) * 2 + core
    quarter = master.shape[1]
    width = grads.shape[3] * 2 // n
    chunks = [(r, a) for r in range(2) for a in range(2)]

    def rows_of(dp_at, a=0, size=quarter):
        return pl.ds(pl.multiple_of(dp_at * quarter + a * TILE, TILE), size)

    loads = [
        pltpu.make_async_copy(src.at[0], state.at[i], load_sem.at[i])
        for i, src in enumerate((master, moment, second))
    ]
    loads += [
        pltpu.make_async_copy(
            grads.at[0, :, rows_of((1 - x) * 2 + core)], own.at[0], load_sem.at[3]
        ),
        pltpu.make_async_copy(grads.at[0, :, rows_of(dp)], own.at[1], load_sem.at[4]),
    ]
    for load in loads:
        load.start()

    barrier = pltpu.get_barrier_semaphore()
    for d in range(1, n):
        pl.semaphore_signal(
            barrier, inc=1, device_id={"expert": lax.rem(me + d, n)}, device_id_type=MESH
        )
    for other in (near, far):
        pl.semaphore_signal(barrier, inc=1, device_id={"dp": other}, device_id_type=MESH)
    pl.semaphore_wait(barrier, n + 1)

    core_copies = []
    for half, x_at in ((0, 1 - x), (1, x)):
        for t, (r, a) in enumerate(chunks):
            copy = pltpu.make_async_remote_copy(
                src_ref=grads.at[0, r, rows_of(x_at * 2 + (1 - core), a, TILE)],
                dst_ref=core_in.at[half, r, pl.ds(a * TILE, TILE)],
                send_sem=core_sem.at[0, half, t],
                recv_sem=core_sem.at[1, half, t],
                device_id={"dp": near},
                device_id_type=MESH,
            )
            copy.start()
            core_copies.append(copy)

    for load in loads[:3]:
        load.wait()
    state_out[...] = state[...].astype(BF16)
    state_copies = []
    for d in range(1, n):
        j = lax.rem(me + d, n)
        rows, cols = piece_at(j, width)
        copy = pltpu.make_async_remote_copy(
            src_ref=state_out.at[:, rows, cols],
            dst_ref=pieces_in.at[me],
            send_sem=state_send.at[d],
            recv_sem=state_recv.at[me],
            device_id={"expert": j},
            device_id_type=MESH,
        )
        copy.start()
        state_copies.append(copy)
    my_rows, my_cols = piece_at(me, width)
    pltpu.make_async_copy(
        state_out.at[:, my_rows, my_cols], pieces_in.at[me], state_recv.at[me]
    ).start()

    loads[3].wait()
    cross_copies = []
    for t, (r, a) in enumerate(chunks):
        core_copies[t].wait_recv()
        at = pl.ds(a * TILE, TILE)
        cross_out[r, at] = (own[0, r, at].astype(F32) + core_in[0, r, at].astype(F32)).astype(BF16)
        copy = pltpu.make_async_remote_copy(
            src_ref=cross_out.at[r, at],
            dst_ref=cross_in.at[r, at],
            send_sem=cross_sem.at[0, t],
            recv_sem=cross_sem.at[1, t],
            device_id={"dp": far},
            device_id_type=MESH,
        )
        copy.start()
        cross_copies.append(copy)

    loads[4].wait()
    for t, (r, a) in enumerate(chunks):
        core_copies[4 + t].wait_recv()
        cross_copies[t].wait_recv()
        at = pl.ds(a * TILE, TILE)
        summed[r, at] = (
            own[1, r, at].astype(F32)
            + core_in[1, r, at].astype(F32)
            + cross_in[r, at].astype(F32)
        ).astype(BF16)
        for high in range(2):
            for side in range(2):
                j = 4 * ((me // 4 + 1 + high) % 2) + 2 * a + (me % 2 + side) % 2
                rows, cols = piece_at(j, width)

                @pl.when(j != me)
                def _():
                    pltpu.make_async_remote_copy(
                        src_ref=summed.at[r, at, cols],
                        dst_ref=incoming.at[me, r],
                        send_sem=part_send.at[j, r],
                        recv_sem=part_recv.at[me, r],
                        device_id={"expert": j},
                        device_id_type=MESH,
                    ).start()

                @pl.when(j == me)
                def _():
                    pltpu.make_async_copy(
                        summed.at[r, at, cols], incoming.at[me, r], part_recv.at[me, r]
                    ).start()

    holds = [
        [owner_slot[old_place[e, r]] for e in range(n)] for r in range(2)
    ]

    def sum_of(r, k):
        total = None
        for e in range(n):
            weight = jnp.where(holds[r][e] == k, 1.0, 0.0).astype(F32)
            term = weight * incoming[e, r].astype(F32)
            total = term if total is None else total + term
        return total

    def wait_parts(r):
        for e in range(n):
            pltpu.make_async_copy(incoming.at[e, r], incoming.at[e, r], part_recv.at[e, r]).wait()

    wait_parts(0)

    @pl.loop(0, n)
    def _(k):
        acc[k] = sum_of(0, k)

    wait_parts(1)

    @pl.loop(0, n)
    def _(d):
        k = lax.rem(me + d + 1, n)
        acc[k] = acc[k] + sum_of(1, k)
        to_owner[k] = acc[k].astype(BF16)

        @pl.when(k != me)
        def _():
            pltpu.make_async_remote_copy(
                src_ref=to_owner.at[k],
                dst_ref=slot_grad.at[my_rows, my_cols],
                send_sem=owner_send.at[k],
                recv_sem=owner_recv.at[me],
                device_id={"expert": k},
                device_id_type=MESH,
            ).start()

        @pl.when(k == me)
        def _():
            pltpu.make_async_copy(
                to_owner.at[k], slot_grad.at[my_rows, my_cols], owner_recv.at[me]
            ).start()

    for e in range(n):
        pltpu.make_async_copy(pieces_in.at[e], pieces_in.at[e], state_recv.at[e]).wait()

    @pl.loop(0, n)
    def _(k):
        fresh[k] = adam(
            pieces_in[k, 0].astype(F32),
            pieces_in[k, 1].astype(F32),
            pieces_in[k, 2].astype(F32),
            acc[k],
        )[0].astype(BF16)

    for d in range(1, n + 1):
        j = lax.rem(me + d, n)
        for r in range(2):
            outbound[j, r] = fresh[owner_slot[new_place[j, r]]]
        if d < n:
            pltpu.make_async_remote_copy(
                src_ref=outbound.at[j],
                dst_ref=replicas.at[:, my_rows, my_cols],
                send_sem=fresh_send.at[j],
                recv_sem=fresh_recv.at[me],
                device_id={"expert": j},
                device_id_type=MESH,
            ).start()
        else:
            pltpu.make_async_copy(
                outbound.at[j], replicas.at[:, my_rows, my_cols], fresh_recv.at[me]
            ).start()

    for e in range(n):
        rows, cols = piece_at(e, width)
        pltpu.make_async_copy(to_owner.at[e], slot_grad.at[rows, cols], owner_recv.at[e]).wait()
        pltpu.make_async_copy(outbound.at[e], replicas.at[:, rows, cols], fresh_recv.at[e]).wait()
    for copy in core_copies + state_copies + cross_copies:
        copy.wait_send()
    for d in range(1, n):
        j = lax.rem(me + d, n)
        for r in range(2):
            pltpu.make_async_copy(incoming.at[j, r], incoming.at[j, r], part_send.at[j, r]).wait()
        pltpu.make_async_copy(to_owner.at[j], to_owner.at[j], owner_send.at[j]).wait()
        pltpu.make_async_copy(outbound.at[j], outbound.at[j], fresh_send.at[j]).wait()


def by_kernel(grads, master, moment, second, old_place, new_place, owner_slot):
    n = lax.axis_size("expert")
    quarter, cols = master.shape[1:]
    width = cols * 2 // n
    dma = pltpu.SemaphoreType.DMA
    any_spec = pl.BlockSpec(memory_space=pl.ANY)
    smem_spec = pl.BlockSpec(memory_space=pltpu.SMEM)
    slot_grad, replicas = pl.pallas_call(
        functools.partial(kernel, n),
        out_shape=(
            jax.ShapeDtypeStruct((quarter, cols), BF16),
            jax.ShapeDtypeStruct((2, quarter, cols), BF16),
        ),
        in_specs=[any_spec] * 4 + [smem_spec] * 3,
        out_specs=(any_spec, any_spec),
        scratch_shapes=[
            pltpu.VMEM((2, 2, quarter, cols), BF16),
            pltpu.VMEM((2, 2, quarter, cols), BF16),
            pltpu.VMEM((2, quarter, cols), BF16),
            pltpu.VMEM((2, quarter, cols), BF16),
            pltpu.VMEM((2, quarter, cols), BF16),
            pltpu.VMEM((n, 2, TILE, width), BF16),
            pltpu.VMEM((n, TILE, width), F32),
            pltpu.VMEM((n, TILE, width), BF16),
            pltpu.VMEM((3, quarter, cols), F32),
            pltpu.VMEM((3, quarter, cols), BF16),
            pltpu.VMEM((n, 3, TILE, width), BF16),
            pltpu.VMEM((n, TILE, width), BF16),
            pltpu.VMEM((n, 2, TILE, width), BF16),
            dma((5,)),
            dma((2, 2, 4)),
            dma((2, 4)),
            dma((n, 2)),
            dma((n, 2)),
            dma((n,)),
            dma((n,)),
            dma((n,)),
            dma((n,)),
            dma((n,)),
            dma((n,)),
        ],
        compiler_params=pltpu.CompilerParams(collective_id=0, has_side_effects=True),
        name="reduce_update_refresh",
    )(grads, master, moment, second, old_place, new_place, owner_slot)
    new_master, new_moment, new_second = adam(master, moment, second, slot_grad[None].astype(F32))
    return (new_master, new_moment, new_second, replicas)


def by_collectives(grads, master, moment, second, old_place, new_place, owner_slot):
    device_count = lax.axis_size("expert")
    slot_count = grads.shape[1]
    col_count = grads.shape[3]
    own_count = master.shape[0]
    quarter_rows = master.shape[1]
    piece_size = quarter_rows * col_count // device_count
    expert_count = owner_slot.shape[0]
    expert_ids = jnp.arange(expert_count, dtype=jnp.int32)
    old_hot = (expert_ids[:, None] == old_place.T.reshape(-1)[None, :]).astype(jnp.float32)
    summed = lax.psum_scatter(
        grads[0].astype(jnp.float32).astype(jnp.bfloat16), "dp", scatter_dimension=1, tiled=True
    ).astype(jnp.float32)
    incoming = lax.all_to_all(
        summed.reshape(slot_count, device_count, piece_size),
        "expert",
        split_axis=1,
        concat_axis=1,
        tiled=True,
    )
    expert_part = jnp.dot(
        old_hot,
        incoming.reshape(slot_count * device_count, piece_size),
        precision=lax.Precision.HIGHEST,
    )
    slot_ids = jnp.arange(device_count * own_count, dtype=jnp.int32)
    owner_hot = (
        (slot_ids[:, None] == owner_slot[None, :])
        .astype(jnp.float32)
        .reshape(device_count, own_count, expert_count)
    )
    outgoing = jnp.einsum("koe,ep->okp", owner_hot, expert_part, precision=lax.Precision.HIGHEST)
    slot_grad = lax.all_to_all(outgoing, "expert", split_axis=1, concat_axis=1, tiled=True).reshape(
        own_count, quarter_rows, col_count
    )
    new_master, new_moment, new_second = adam(master, moment, second, slot_grad)
    fresh = new_master.astype(jnp.bfloat16).reshape(own_count, device_count, piece_size)
    every_slot = lax.all_to_all(fresh, "expert", split_axis=1, concat_axis=0, tiled=True).reshape(
        device_count * own_count, piece_size
    )
    wanted = owner_slot[new_place.T.reshape(-1)]
    outbound = jnp.take(every_slot, wanted, axis=0).reshape(slot_count, device_count, piece_size)
    received = lax.all_to_all(outbound, "expert", split_axis=1, concat_axis=1, tiled=True)
    replicas = received.reshape(slot_count, quarter_rows, col_count)
    return (new_master, new_moment, new_second, replicas)


def on_device(grads, master, moment, second, old_place, new_place, owner_slot):
    fits = (
        lax.axis_size("dp") == 4
        and lax.axis_size("expert") == 8
        and grads.shape[1] == 2
        and master.shape[0] == 1
        and owner_slot.shape[0] == 8
        and master.shape[1] == 2 * TILE
        and grads.shape[3] % (4 * 128) == 0
    )
    plan = by_kernel if fits else by_collectives
    return plan(grads, master, moment, second, old_place, new_place, owner_slot)


def solution(mesh):
    placed = (
        P("dp", "expert", None, None),
        P("expert", "dp", None),
        P("expert", "dp", None),
        P("expert", "dp", None),
        P(),
        P(),
        P(),
    )
    return jax.shard_map(
        on_device,
        mesh=mesh,
        in_specs=placed,
        out_specs=(
            P("expert", "dp", None),
            P("expert", "dp", None),
            P("expert", "dp", None),
            P("expert", "dp", None),
        ),
        check_vma=False,
    )
```

```python
import functools

import jax
import jax.numpy as jnp
from jax import lax
from jax.experimental import pallas as pl
from jax.experimental.pallas import tpu as pltpu
from jax.sharding import PartitionSpec as P

beta_first = 0.9
beta_second = 0.999
learn_rate = 0.02
weight_decay = 0.1
epsilon = 1e-08
scale_first = 1.0 - 0.9**40
scale_second = 1.0 - 0.999**40
MESH = pl.DeviceIdType.MESH
F32 = jnp.float32
BF16 = jnp.bfloat16
TILE = 16


def adam(master, moment, second, grad):
    new_moment = beta_first * moment + (1.0 - beta_first) * grad
    new_second = beta_second * second + (1.0 - beta_second) * grad * grad
    update = new_moment / scale_first / (jnp.sqrt(new_second / scale_second) + epsilon)
    new_master = master - learn_rate * (update + weight_decay * master)
    return new_master, new_moment, new_second


def piece_at(j, width):
    rows = pl.ds(pl.multiple_of(((j // 2) % 2) * TILE, TILE), TILE)
    cols = pl.ds(pl.multiple_of(((j // 4) * 2 + j % 2) * width, 128), width)
    return rows, cols


def kernel(
    n,
    grads,
    master,
    moment,
    second,
    old_place,
    new_place,
    owner_slot,
    slot_grad,
    replicas,
    own,
    core_in,
    cross_out,
    cross_in,
    summed,
    incoming,
    acc,
    to_owner,
    state,
    state_out,
    pieces_in,
    fresh,
    outbound,
    load_sem,
    core_sem,
    cross_sem,
    part_send,
    part_recv,
    state_send,
    state_recv,
    owner_send,
    owner_recv,
    fresh_send,
    fresh_recv,
):
    me = lax.axis_index("expert")
    dp = lax.axis_index("dp")
    x, core = dp // 2, dp % 2
    near = x * 2 + (1 - core)
    far = (1 - x) * 2 + core
    quarter = master.shape[1]
    width = grads.shape[3] * 2 // n
    chunks = [(r, a) for r in range(2) for a in range(2)]

    def rows_of(dp_at, a=0, size=quarter):
        return pl.ds(pl.multiple_of(dp_at * quarter + a * TILE, TILE), size)

    loads = [
        pltpu.make_async_copy(src.at[0], state.at[i], load_sem.at[i])
        for i, src in enumerate((master, moment, second))
    ]
    loads += [
        pltpu.make_async_copy(
            grads.at[0, :, rows_of((1 - x) * 2 + core)], own.at[0], load_sem.at[3]
        ),
        pltpu.make_async_copy(grads.at[0, :, rows_of(dp)], own.at[1], load_sem.at[4]),
    ]
    for load in loads:
        load.start()

    barrier = pltpu.get_barrier_semaphore()
    for d in range(1, n):
        pl.semaphore_signal(
            barrier, inc=1, device_id={"expert": lax.rem(me + d, n)}, device_id_type=MESH
        )
    for other in (near, far):
        pl.semaphore_signal(barrier, inc=1, device_id={"dp": other}, device_id_type=MESH)
    pl.semaphore_wait(barrier, n + 1)

    core_copies = []
    for half, x_at in ((0, 1 - x), (1, x)):
        for t, (r, a) in enumerate(chunks):
            copy = pltpu.make_async_remote_copy(
                src_ref=grads.at[0, r, rows_of(x_at * 2 + (1 - core), a, TILE)],
                dst_ref=core_in.at[half, r, pl.ds(a * TILE, TILE)],
                send_sem=core_sem.at[0, half, t],
                recv_sem=core_sem.at[1, half, t],
                device_id={"dp": near},
                device_id_type=MESH,
            )
            copy.start()
            core_copies.append(copy)

    for load in loads[:3]:
        load.wait()
    state_out[...] = state[...].astype(BF16)
    state_copies = []
    my_rows, my_cols = piece_at(me, width)

    def send_state(first, count):
        part = pl.ds(first, count)
        for d in range(1, n):
            j = lax.rem(me + d, n)
            rows, cols = piece_at(j, width)
            copy = pltpu.make_async_remote_copy(
                src_ref=state_out.at[part, rows, cols],
                dst_ref=pieces_in.at[me, part],
                send_sem=state_send.at[d, first],
                recv_sem=state_recv.at[me, first],
                device_id={"expert": j},
                device_id_type=MESH,
            )
            copy.start()
            state_copies.append(copy)
        pltpu.make_async_copy(
            state_out.at[part, my_rows, my_cols], pieces_in.at[me, part], state_recv.at[me, first]
        ).start()

    def wait_state(first, count):
        part = pl.ds(first, count)
        for e in range(n):
            piece = pieces_in.at[e, part]
            pltpu.make_async_copy(piece, piece, state_recv.at[e, first]).wait()

    send_state(0, 2)

    loads[3].wait()
    cross_copies = []
    for t, (r, a) in enumerate(chunks):
        core_copies[t].wait_recv()
        at = pl.ds(a * TILE, TILE)
        cross_out[r, at] = (own[0, r, at].astype(F32) + core_in[0, r, at].astype(F32)).astype(BF16)
        copy = pltpu.make_async_remote_copy(
            src_ref=cross_out.at[r, at],
            dst_ref=cross_in.at[r, at],
            send_sem=cross_sem.at[0, t],
            recv_sem=cross_sem.at[1, t],
            device_id={"dp": far},
            device_id_type=MESH,
        )
        copy.start()
        cross_copies.append(copy)

    loads[4].wait()
    for t, (r, a) in enumerate(chunks):
        core_copies[4 + t].wait_recv()
        cross_copies[t].wait_recv()
        at = pl.ds(a * TILE, TILE)
        summed[r, at] = (
            own[1, r, at].astype(F32)
            + core_in[1, r, at].astype(F32)
            + cross_in[r, at].astype(F32)
        ).astype(BF16)
        for high in range(2):
            for side in range(2):
                j = 4 * ((me // 4 + 1 + high) % 2) + 2 * a + (me % 2 + side) % 2
                rows, cols = piece_at(j, width)

                @pl.when(j != me)
                def _():
                    pltpu.make_async_remote_copy(
                        src_ref=summed.at[r, at, cols],
                        dst_ref=incoming.at[me, r],
                        send_sem=part_send.at[j, r],
                        recv_sem=part_recv.at[me, r],
                        device_id={"expert": j},
                        device_id_type=MESH,
                    ).start()

                @pl.when(j == me)
                def _():
                    pltpu.make_async_copy(
                        summed.at[r, at, cols], incoming.at[me, r], part_recv.at[me, r]
                    ).start()

    send_state(2, 1)

    holds = [
        [owner_slot[old_place[r, e]] for e in range(n)] for r in range(2)
    ]

    def sum_of(r, k):
        total = None
        for e in range(n):
            weight = jnp.where(holds[r][e] == k, 1.0, 0.0).astype(F32)
            term = weight * incoming[e, r].astype(F32)
            total = term if total is None else total + term
        return total

    def wait_parts(r):
        for e in range(n):
            pltpu.make_async_copy(incoming.at[e, r], incoming.at[e, r], part_recv.at[e, r]).wait()

    wait_parts(0)

    @pl.loop(0, n)
    def _(k):
        acc[k] = sum_of(0, k)

    wait_parts(1)

    @pl.loop(0, n)
    def _(d):
        k = lax.rem(me + d + 1, n)
        acc[k] = acc[k] + sum_of(1, k)
        to_owner[k] = acc[k].astype(BF16)

        @pl.when(k != me)
        def _():
            pltpu.make_async_remote_copy(
                src_ref=to_owner.at[k],
                dst_ref=slot_grad.at[my_rows, my_cols],
                send_sem=owner_send.at[k],
                recv_sem=owner_recv.at[me],
                device_id={"expert": k},
                device_id_type=MESH,
            ).start()

        @pl.when(k == me)
        def _():
            pltpu.make_async_copy(
                to_owner.at[k], slot_grad.at[my_rows, my_cols], owner_recv.at[me]
            ).start()

    wait_state(0, 2)
    wait_state(2, 1)

    @pl.loop(0, n)
    def _(k):
        fresh[k] = adam(
            pieces_in[k, 0].astype(F32),
            pieces_in[k, 1].astype(F32),
            pieces_in[k, 2].astype(F32),
            acc[k],
        )[0].astype(BF16)

    for d in range(1, n + 1):
        j = lax.rem(me + d, n)
        for r in range(2):
            outbound[j, r] = fresh[owner_slot[new_place[r, j]]]
        if d < n:
            pltpu.make_async_remote_copy(
                src_ref=outbound.at[j],
                dst_ref=replicas.at[:, my_rows, my_cols],
                send_sem=fresh_send.at[j],
                recv_sem=fresh_recv.at[me],
                device_id={"expert": j},
                device_id_type=MESH,
            ).start()
        else:
            pltpu.make_async_copy(
                outbound.at[j], replicas.at[:, my_rows, my_cols], fresh_recv.at[me]
            ).start()

    for e in range(n):
        rows, cols = piece_at(e, width)
        pltpu.make_async_copy(to_owner.at[e], slot_grad.at[rows, cols], owner_recv.at[e]).wait()
        pltpu.make_async_copy(outbound.at[e], replicas.at[:, rows, cols], fresh_recv.at[e]).wait()
    for copy in core_copies + state_copies + cross_copies:
        copy.wait_send()
    for d in range(1, n):
        j = lax.rem(me + d, n)
        for r in range(2):
            pltpu.make_async_copy(incoming.at[j, r], incoming.at[j, r], part_send.at[j, r]).wait()
        pltpu.make_async_copy(to_owner.at[j], to_owner.at[j], owner_send.at[j]).wait()
        pltpu.make_async_copy(outbound.at[j], outbound.at[j], fresh_send.at[j]).wait()


def by_kernel(grads, master, moment, second, old_place, new_place, owner_slot):
    n = lax.axis_size("expert")
    quarter, cols = master.shape[1:]
    width = cols * 2 // n
    dma = pltpu.SemaphoreType.DMA
    any_spec = pl.BlockSpec(memory_space=pl.ANY)
    smem_spec = pl.BlockSpec(memory_space=pltpu.SMEM)
    slot_grad, replicas = pl.pallas_call(
        functools.partial(kernel, n),
        out_shape=(
            jax.ShapeDtypeStruct((quarter, cols), BF16),
            jax.ShapeDtypeStruct((2, quarter, cols), BF16),
        ),
        in_specs=[any_spec] * 4 + [smem_spec] * 3,
        out_specs=(any_spec, any_spec),
        scratch_shapes=[
            pltpu.VMEM((2, 2, quarter, cols), BF16),
            pltpu.VMEM((2, 2, quarter, cols), BF16),
            pltpu.VMEM((2, quarter, cols), BF16),
            pltpu.VMEM((2, quarter, cols), BF16),
            pltpu.VMEM((2, quarter, cols), BF16),
            pltpu.VMEM((n, 2, TILE, width), BF16),
            pltpu.VMEM((n, TILE, width), F32),
            pltpu.VMEM((n, TILE, width), BF16),
            pltpu.VMEM((3, quarter, cols), F32),
            pltpu.VMEM((3, quarter, cols), BF16),
            pltpu.VMEM((n, 3, TILE, width), BF16),
            pltpu.VMEM((n, TILE, width), BF16),
            pltpu.VMEM((n, 2, TILE, width), BF16),
            dma((5,)),
            dma((2, 2, 4)),
            dma((2, 4)),
            dma((n, 2)),
            dma((n, 2)),
            dma((n, 3)),
            dma((n, 3)),
            dma((n,)),
            dma((n,)),
            dma((n,)),
            dma((n,)),
        ],
        compiler_params=pltpu.CompilerParams(collective_id=0, has_side_effects=True),
        name="reduce_update_refresh",
    )(grads, master, moment, second, old_place.T, new_place.T, owner_slot)
    new_master, new_moment, new_second = adam(master, moment, second, slot_grad[None].astype(F32))
    return (new_master, new_moment, new_second, replicas)


def by_collectives(grads, master, moment, second, old_place, new_place, owner_slot):
    device_count = lax.axis_size("expert")
    slot_count = grads.shape[1]
    col_count = grads.shape[3]
    own_count = master.shape[0]
    quarter_rows = master.shape[1]
    piece_size = quarter_rows * col_count // device_count
    expert_count = owner_slot.shape[0]
    expert_ids = jnp.arange(expert_count, dtype=jnp.int32)
    old_hot = (expert_ids[:, None] == old_place.T.reshape(-1)[None, :]).astype(jnp.float32)
    summed = lax.psum_scatter(
        grads[0].astype(jnp.float32).astype(jnp.bfloat16), "dp", scatter_dimension=1, tiled=True
    ).astype(jnp.float32)
    incoming = lax.all_to_all(
        summed.reshape(slot_count, device_count, piece_size),
        "expert",
        split_axis=1,
        concat_axis=1,
        tiled=True,
    )
    expert_part = jnp.dot(
        old_hot,
        incoming.reshape(slot_count * device_count, piece_size),
        precision=lax.Precision.HIGHEST,
    )
    slot_ids = jnp.arange(device_count * own_count, dtype=jnp.int32)
    owner_hot = (
        (slot_ids[:, None] == owner_slot[None, :])
        .astype(jnp.float32)
        .reshape(device_count, own_count, expert_count)
    )
    outgoing = jnp.einsum("koe,ep->okp", owner_hot, expert_part, precision=lax.Precision.HIGHEST)
    slot_grad = lax.all_to_all(outgoing, "expert", split_axis=1, concat_axis=1, tiled=True).reshape(
        own_count, quarter_rows, col_count
    )
    new_master, new_moment, new_second = adam(master, moment, second, slot_grad)
    fresh = new_master.astype(jnp.bfloat16).reshape(own_count, device_count, piece_size)
    every_slot = lax.all_to_all(fresh, "expert", split_axis=1, concat_axis=0, tiled=True).reshape(
        device_count * own_count, piece_size
    )
    wanted = owner_slot[new_place.T.reshape(-1)]
    outbound = jnp.take(every_slot, wanted, axis=0).reshape(slot_count, device_count, piece_size)
    received = lax.all_to_all(outbound, "expert", split_axis=1, concat_axis=1, tiled=True)
    replicas = received.reshape(slot_count, quarter_rows, col_count)
    return (new_master, new_moment, new_second, replicas)


def on_device(grads, master, moment, second, old_place, new_place, owner_slot):
    fits = (
        lax.axis_size("dp") == 4
        and lax.axis_size("expert") == 8
        and grads.shape[1] == 2
        and master.shape[0] == 1
        and owner_slot.shape[0] == 8
        and master.shape[1] == 2 * TILE
        and grads.shape[3] % (4 * 128) == 0
    )
    plan = by_kernel if fits else by_collectives
    return plan(grads, master, moment, second, old_place, new_place, owner_slot)


def solution(mesh):
    placed = (
        P("dp", "expert", None, None),
        P("expert", "dp", None),
        P("expert", "dp", None),
        P("expert", "dp", None),
        P(),
        P(),
        P(),
    )
    return jax.shard_map(
        on_device,
        mesh=mesh,
        in_specs=placed,
        out_specs=(
            P("expert", "dp", None),
            P("expert", "dp", None),
            P("expert", "dp", None),
            P("expert", "dp", None),
        ),
        check_vma=False,
    )
```

```python
import functools

import jax
import jax.numpy as jnp
from jax import lax
from jax.experimental import pallas as pl
from jax.experimental.pallas import tpu as pltpu
from jax.sharding import PartitionSpec as P

beta_first = 0.9
beta_second = 0.999
learn_rate = 0.02
weight_decay = 0.1
epsilon = 1e-08
scale_first = 1.0 - 0.9**40
scale_second = 1.0 - 0.999**40
MESH = pl.DeviceIdType.MESH
F32 = jnp.float32
BF16 = jnp.bfloat16
TILE = 16


def adam(master, moment, second, grad):
    new_moment = beta_first * moment + (1.0 - beta_first) * grad
    new_second = beta_second * second + (1.0 - beta_second) * grad * grad
    update = new_moment / scale_first / (jnp.sqrt(new_second / scale_second) + epsilon)
    new_master = master - learn_rate * (update + weight_decay * master)
    return new_master, new_moment, new_second


def piece_at(j, width):
    rows = pl.ds(pl.multiple_of(((j // 2) % 2) * TILE, TILE), TILE)
    cols = pl.ds(pl.multiple_of(((j // 4) * 2 + j % 2) * width, 128), width)
    return rows, cols


def kernel(
    n,
    grads,
    master,
    moment,
    second,
    old_place,
    new_place,
    owner_slot,
    new_master,
    new_moment,
    new_second,
    replicas,
    own,
    core_in,
    cross_out,
    cross_in,
    summed,
    incoming,
    acc,
    to_owner,
    slot_grad,
    state,
    state_out,
    pieces_in,
    fresh,
    outbound,
    load_sem,
    store_sem,
    core_send,
    core_recv,
    cross_send,
    cross_recv,
    part_send,
    part_recv,
    state_send,
    state_recv,
    owner_sem,
    fresh_sem,
):
    me = lax.axis_index("expert")
    dp = lax.axis_index("dp")
    x, core = dp // 2, dp % 2
    near = x * 2 + (1 - core)
    far = (1 - x) * 2 + core
    quarter = master.shape[1]
    width = grads.shape[3] * 2 // n
    chunks = [(r, a) for r in range(2) for a in range(2)]

    def rows_of(dp_at, a=0, size=quarter):
        return pl.ds(pl.multiple_of(dp_at * quarter + a * TILE, TILE), size)

    def wait_bytes(ref, sem):
        pltpu.make_async_copy(ref, ref, sem).wait()

    def send(src, dst, send_sem, recv_sem, to):
        pltpu.make_async_remote_copy(
            src_ref=src,
            dst_ref=dst,
            send_sem=send_sem,
            recv_sem=recv_sem,
            device_id=to,
            device_id_type=MESH,
        ).start()

    loads = [
        pltpu.make_async_copy(src.at[0], state.at[i], load_sem.at[i])
        for i, src in enumerate((master, moment, second))
    ]
    loads += [
        pltpu.make_async_copy(
            grads.at[0, :, rows_of((1 - x) * 2 + core)], own.at[0], load_sem.at[3]
        ),
        pltpu.make_async_copy(grads.at[0, :, rows_of(dp)], own.at[1], load_sem.at[4]),
    ]
    barrier = pltpu.get_barrier_semaphore()
    for d in range(1, n):
        pl.semaphore_signal(
            barrier, inc=1, device_id={"expert": lax.rem(me + d, n)}, device_id_type=MESH
        )
    for other in (near, far):
        pl.semaphore_signal(barrier, inc=1, device_id={"dp": other}, device_id_type=MESH)
    for load in loads:
        load.start()
    for i in range(3):
        loads[i].wait()
        state_out[i] = state[i].astype(BF16)
    pl.semaphore_wait(barrier, n + 1)

    for half, x_at in ((0, 1 - x), (1, x)):
        for t, (r, a) in enumerate(chunks):
            send(
                grads.at[0, r, rows_of(x_at * 2 + (1 - core), a, TILE)],
                core_in.at[half, r, pl.ds(a * TILE, TILE)],
                core_send,
                core_recv.at[half, t],
                {"dp": near},
            )

    my_rows, my_cols = piece_at(me, width)

    def send_state(first, count):
        part = pl.ds(first, count)
        for d in range(1, n):
            j = lax.rem(me + d, n)
            rows, cols = piece_at(j, width)
            send(
                state_out.at[part, rows, cols],
                pieces_in.at[me, part],
                state_send.at[first],
                state_recv.at[first],
                {"expert": j},
            )
        pltpu.make_async_copy(
            state_out.at[part, my_rows, my_cols], pieces_in.at[me, part], state_recv.at[first]
        ).start()

    send_state(0, 2)

    loads[3].wait()
    for t, (r, a) in enumerate(chunks):
        at = pl.ds(a * TILE, TILE)
        wait_bytes(core_in.at[0, r, at], core_recv.at[0, t])
        cross_out[r, at] = (own[0, r, at].astype(F32) + core_in[0, r, at].astype(F32)).astype(BF16)
        send(cross_out.at[r, at], cross_in.at[r, at], cross_send, cross_recv.at[t], {"dp": far})

    loads[4].wait()
    for t, (r, a) in enumerate(chunks):
        at = pl.ds(a * TILE, TILE)
        wait_bytes(core_in.at[1, r, at], core_recv.at[1, t])
        wait_bytes(cross_in.at[r, at], cross_recv.at[t])
        summed[r, at] = (
            own[1, r, at].astype(F32)
            + core_in[1, r, at].astype(F32)
            + cross_in[r, at].astype(F32)
        ).astype(BF16)
        for high in range(2):
            for side in range(2):
                j = 4 * ((me // 4 + 1 + high) % 2) + 2 * a + (me % 2 + side) % 2
                rows, cols = piece_at(j, width)

                @pl.when(j != me)
                def _():
                    send(
                        summed.at[r, at, cols],
                        incoming.at[r, me],
                        part_send.at[r],
                        part_recv.at[r],
                        {"expert": j},
                    )

                @pl.when(j == me)
                def _():
                    pltpu.make_async_copy(
                        summed.at[r, at, cols], incoming.at[r, me], part_recv.at[r]
                    ).start()

    send_state(2, 1)

    holds = [[owner_slot[old_place[r, e]] for e in range(n)] for r in range(2)]

    def sum_of(r, k):
        total = None
        for e in range(n):
            weight = jnp.where(holds[r][e] == k, 1.0, 0.0).astype(F32)
            term = weight * incoming[r, e].astype(F32)
            total = term if total is None else total + term
        return total

    wait_bytes(incoming.at[0], part_recv.at[0])

    @pl.loop(0, n)
    def _(k):
        acc[k] = sum_of(0, k)

    wait_bytes(incoming.at[1], part_recv.at[1])

    @pl.loop(0, n)
    def _(d):
        k = lax.rem(me + d + 1, n)
        acc[k] = acc[k] + sum_of(1, k)
        to_owner[k] = acc[k].astype(BF16)

        @pl.when(k != me)
        def _():
            send(
                to_owner.at[k],
                slot_grad.at[my_rows, my_cols],
                owner_sem.at[0],
                owner_sem.at[1],
                {"expert": k},
            )

        @pl.when(k == me)
        def _():
            pltpu.make_async_copy(
                to_owner.at[k], slot_grad.at[my_rows, my_cols], owner_sem.at[1]
            ).start()

    wait_bytes(pieces_in.at[:, pl.ds(0, 2)], state_recv.at[0])
    wait_bytes(pieces_in.at[:, pl.ds(2, 1)], state_recv.at[2])

    @pl.loop(0, n)
    def _(k):
        fresh[k] = adam(
            pieces_in[k, 0].astype(F32),
            pieces_in[k, 1].astype(F32),
            pieces_in[k, 2].astype(F32),
            acc[k],
        )[0].astype(BF16)

    for d in range(1, n + 1):
        j = lax.rem(me + d, n)
        for r in range(2):
            outbound[j, r] = fresh[owner_slot[new_place[r, j]]]
        there = replicas.at[:, my_rows, my_cols]
        if d < n:
            send(outbound.at[j], there, fresh_sem.at[0], fresh_sem.at[1], {"expert": j})
        else:
            pltpu.make_async_copy(outbound.at[j], there, fresh_sem.at[1]).start()

    wait_bytes(slot_grad, owner_sem.at[1])

    @pl.loop(0, n)
    def _(e):
        rows, cols = piece_at(e, width)
        result = adam(
            state[0, rows, cols],
            state[1, rows, cols],
            state[2, rows, cols],
            slot_grad[rows, cols].astype(F32),
        )
        for i in range(3):
            state[i, rows, cols] = result[i]

    stores = [
        pltpu.make_async_copy(state.at[i], dst.at[0], store_sem.at[i])
        for i, dst in enumerate((new_master, new_moment, new_second))
    ]
    for store in stores:
        store.start()

    others = pl.ds(0, n - 1)
    wait_bytes(own, core_send)
    wait_bytes(cross_out, cross_send)
    wait_bytes(pieces_in.at[others, pl.ds(0, 2)], state_send.at[0])
    wait_bytes(pieces_in.at[others, pl.ds(2, 1)], state_send.at[2])
    for r in range(2):
        wait_bytes(incoming.at[r, others], part_send.at[r])
    wait_bytes(to_owner.at[others], owner_sem.at[0])
    for store in stores:
        store.wait()
    wait_bytes(outbound.at[others], fresh_sem.at[0])
    wait_bytes(replicas, fresh_sem.at[1])


def hand_over(*refs):
    count = len(refs) // 2
    copies = [
        pltpu.make_async_copy(refs[i], refs[count + i], refs[-1].at[i]) for i in range(count)
    ]
    for copy in copies:
        copy.start()
    for copy in copies:
        copy.wait()


def by_kernel(grads, master, moment, second, old_place, new_place, owner_slot):
    n = lax.axis_size("expert")
    quarter, cols = master.shape[1:]
    width = cols * 2 // n
    dma = pltpu.SemaphoreType.DMA
    any_spec = pl.BlockSpec(memory_space=pl.ANY)
    smem_spec = pl.BlockSpec(memory_space=pltpu.SMEM)
    out_shape = (jax.ShapeDtypeStruct(master.shape, F32),) * 3 + (
        jax.ShapeDtypeStruct((2, quarter, cols), BF16),
    )
    results = pl.pallas_call(
        functools.partial(kernel, n),
        out_shape=out_shape,
        in_specs=[any_spec] * 4 + [smem_spec] * 3,
        out_specs=(any_spec,) * 4,
        scratch_shapes=[
            pltpu.VMEM((2, 2, quarter, cols), BF16),
            pltpu.VMEM((2, 2, quarter, cols), BF16),
            pltpu.VMEM((2, quarter, cols), BF16),
            pltpu.VMEM((2, quarter, cols), BF16),
            pltpu.VMEM((2, quarter, cols), BF16),
            pltpu.VMEM((2, n, TILE, width), BF16),
            pltpu.VMEM((n, TILE, width), F32),
            pltpu.VMEM((n, TILE, width), BF16),
            pltpu.VMEM((quarter, cols), BF16),
            pltpu.VMEM((3, quarter, cols), F32),
            pltpu.VMEM((3, quarter, cols), BF16),
            pltpu.VMEM((n, 3, TILE, width), BF16),
            pltpu.VMEM((n, TILE, width), BF16),
            pltpu.VMEM((n, 2, TILE, width), BF16),
            dma((5,)),
            dma((3,)),
            dma,
            dma((2, 4)),
            dma,
            dma((4,)),
            dma((2,)),
            dma((2,)),
            dma((3,)),
            dma((3,)),
            dma((2,)),
            dma((2,)),
        ],
        compiler_params=pltpu.CompilerParams(collective_id=0, has_side_effects=True),
        name="reduce_update_refresh",
    )(grads, master, moment, second, old_place.T, new_place.T, owner_slot)
    return pl.pallas_call(
        hand_over,
        out_shape=out_shape,
        in_specs=[any_spec] * 4,
        out_specs=(any_spec,) * 4,
        scratch_shapes=[dma((4,))],
        name="hand_over",
    )(*results)


def by_collectives(grads, master, moment, second, old_place, new_place, owner_slot):
    device_count = lax.axis_size("expert")
    slot_count = grads.shape[1]
    col_count = grads.shape[3]
    own_count = master.shape[0]
    quarter_rows = master.shape[1]
    piece_size = quarter_rows * col_count // device_count
    expert_count = owner_slot.shape[0]
    expert_ids = jnp.arange(expert_count, dtype=jnp.int32)
    old_hot = (expert_ids[:, None] == old_place.T.reshape(-1)[None, :]).astype(jnp.float32)
    summed = lax.psum_scatter(
        grads[0].astype(jnp.float32).astype(jnp.bfloat16), "dp", scatter_dimension=1, tiled=True
    ).astype(jnp.float32)
    incoming = lax.all_to_all(
        summed.reshape(slot_count, device_count, piece_size),
        "expert",
        split_axis=1,
        concat_axis=1,
        tiled=True,
    )
    expert_part = jnp.dot(
        old_hot,
        incoming.reshape(slot_count * device_count, piece_size),
        precision=lax.Precision.HIGHEST,
    )
    slot_ids = jnp.arange(device_count * own_count, dtype=jnp.int32)
    owner_hot = (
        (slot_ids[:, None] == owner_slot[None, :])
        .astype(jnp.float32)
        .reshape(device_count, own_count, expert_count)
    )
    outgoing = jnp.einsum("koe,ep->okp", owner_hot, expert_part, precision=lax.Precision.HIGHEST)
    slot_grad = lax.all_to_all(outgoing, "expert", split_axis=1, concat_axis=1, tiled=True).reshape(
        own_count, quarter_rows, col_count
    )
    new_master, new_moment, new_second = adam(master, moment, second, slot_grad)
    fresh = new_master.astype(jnp.bfloat16).reshape(own_count, device_count, piece_size)
    every_slot = lax.all_to_all(fresh, "expert", split_axis=1, concat_axis=0, tiled=True).reshape(
        device_count * own_count, piece_size
    )
    wanted = owner_slot[new_place.T.reshape(-1)]
    outbound = jnp.take(every_slot, wanted, axis=0).reshape(slot_count, device_count, piece_size)
    received = lax.all_to_all(outbound, "expert", split_axis=1, concat_axis=1, tiled=True)
    replicas = received.reshape(slot_count, quarter_rows, col_count)
    return (new_master, new_moment, new_second, replicas)


def on_device(grads, master, moment, second, old_place, new_place, owner_slot):
    fits = (
        lax.axis_size("dp") == 4
        and lax.axis_size("expert") == 8
        and grads.shape[1] == 2
        and master.shape[0] == 1
        and owner_slot.shape[0] == 8
        and master.shape[1] == 2 * TILE
        and grads.shape[3] % (4 * 128) == 0
    )
    plan = by_kernel if fits else by_collectives
    return plan(grads, master, moment, second, old_place, new_place, owner_slot)


def solution(mesh):
    placed = (
        P("dp", "expert", None, None),
        P("expert", "dp", None),
        P("expert", "dp", None),
        P("expert", "dp", None),
        P(),
        P(),
        P(),
    )
    return jax.shard_map(
        on_device,
        mesh=mesh,
        in_specs=placed,
        out_specs=(
            P("expert", "dp", None),
            P("expert", "dp", None),
            P("expert", "dp", None),
            P("expert", "dp", None),
        ),
        check_vma=False,
    )
```

```python
import functools

import jax
import jax.numpy as jnp
from jax import lax
from jax.experimental import pallas as pl
from jax.experimental.pallas import tpu as pltpu
from jax.sharding import PartitionSpec as P

beta_first = 0.9
beta_second = 0.999
learn_rate = 0.02
weight_decay = 0.1
epsilon = 1e-08
scale_first = 1.0 - 0.9**40
scale_second = 1.0 - 0.999**40
MESH = pl.DeviceIdType.MESH
F32 = jnp.float32
BF16 = jnp.bfloat16
TILE = 16


def adam(master, moment, second, grad):
    new_moment = beta_first * moment + (1.0 - beta_first) * grad
    new_second = beta_second * second + (1.0 - beta_second) * grad * grad
    update = new_moment / scale_first / (jnp.sqrt(new_second / scale_second) + epsilon)
    new_master = master - learn_rate * (update + weight_decay * master)
    return new_master, new_moment, new_second


def piece_at(j, width):
    rows = pl.ds(pl.multiple_of(((j // 2) % 2) * TILE, TILE), TILE)
    cols = pl.ds(pl.multiple_of(((j // 4) * 2 + j % 2) * width, 128), width)
    return rows, cols


def kernel(
    n,
    grads,
    master,
    moment,
    second,
    old_place,
    new_place,
    owner_slot,
    new_master,
    new_moment,
    new_second,
    replicas,
    own,
    core_in,
    cross_out,
    cross_in,
    summed,
    incoming,
    acc,
    to_owner,
    slot_grad,
    state,
    state_out,
    pieces_in,
    fresh,
    outbound,
    load_sem,
    core_send,
    core_recv,
    cross_send,
    cross_recv,
    part_send,
    part_recv,
    state_send,
    state_recv,
    owner_sem,
    fresh_sem,
):
    me = lax.axis_index("expert")
    dp = lax.axis_index("dp")
    x, core = dp // 2, dp % 2
    near = x * 2 + (1 - core)
    far = (1 - x) * 2 + core
    quarter = master.shape[1]
    width = grads.shape[3] * 2 // n
    chunks = [(r, a) for r in range(2) for a in range(2)]

    def rows_of(dp_at, a=0, size=quarter):
        return pl.ds(pl.multiple_of(dp_at * quarter + a * TILE, TILE), size)

    def wait_bytes(ref, sem):
        pltpu.make_async_copy(ref, ref, sem).wait()

    def send(src, dst, send_sem, recv_sem, to):
        pltpu.make_async_remote_copy(
            src_ref=src,
            dst_ref=dst,
            send_sem=send_sem,
            recv_sem=recv_sem,
            device_id=to,
            device_id_type=MESH,
        ).start()

    loads = [
        pltpu.make_async_copy(src.at[0], state.at[i], load_sem.at[i])
        for i, src in enumerate((master, moment, second))
    ]
    loads += [
        pltpu.make_async_copy(
            grads.at[0, :, rows_of((1 - x) * 2 + core)], own.at[0], load_sem.at[3]
        ),
        pltpu.make_async_copy(grads.at[0, :, rows_of(dp)], own.at[1], load_sem.at[4]),
    ]
    barrier = pltpu.get_barrier_semaphore()
    for d in range(1, n):
        pl.semaphore_signal(
            barrier, inc=1, device_id={"expert": lax.rem(me + d, n)}, device_id_type=MESH
        )
    for other in (near, far):
        pl.semaphore_signal(barrier, inc=1, device_id={"dp": other}, device_id_type=MESH)
    for load in loads:
        load.start()
    for i in range(3):
        loads[i].wait()
        state_out[i] = state[i].astype(BF16)
    pl.semaphore_wait(barrier, n + 1)

    for half, x_at in ((0, 1 - x), (1, x)):
        for t, (r, a) in enumerate(chunks):
            send(
                grads.at[0, r, rows_of(x_at * 2 + (1 - core), a, TILE)],
                core_in.at[half, r, pl.ds(a * TILE, TILE)],
                core_send,
                core_recv.at[half, t],
                {"dp": near},
            )

    my_rows, my_cols = piece_at(me, width)

    def send_state(first, count):
        part = pl.ds(first, count)
        for d in range(1, n):
            j = lax.rem(me + d, n)
            rows, cols = piece_at(j, width)
            send(
                state_out.at[part, rows, cols],
                pieces_in.at[me, part],
                state_send.at[first],
                state_recv.at[first],
                {"expert": j},
            )
        pltpu.make_async_copy(
            state_out.at[part, my_rows, my_cols], pieces_in.at[me, part], state_recv.at[first]
        ).start()

    send_state(0, 2)

    loads[3].wait()
    for t, (r, a) in enumerate(chunks):
        at = pl.ds(a * TILE, TILE)
        wait_bytes(core_in.at[0, r, at], core_recv.at[0, t])
        cross_out[r, at] = (own[0, r, at].astype(F32) + core_in[0, r, at].astype(F32)).astype(BF16)
        send(cross_out.at[r, at], cross_in.at[r, at], cross_send, cross_recv.at[t], {"dp": far})

    loads[4].wait()
    for t, (r, a) in enumerate(chunks):
        at = pl.ds(a * TILE, TILE)
        wait_bytes(core_in.at[1, r, at], core_recv.at[1, t])
        wait_bytes(cross_in.at[r, at], cross_recv.at[t])
        summed[r, at] = (
            own[1, r, at].astype(F32)
            + core_in[1, r, at].astype(F32)
            + cross_in[r, at].astype(F32)
        ).astype(BF16)
        for high in range(2):
            for side in range(2):
                j = 4 * ((me // 4 + 1 + high) % 2) + 2 * a + (me % 2 + side) % 2
                rows, cols = piece_at(j, width)

                @pl.when(j != me)
                def _():
                    send(
                        summed.at[r, at, cols],
                        incoming.at[r, me],
                        part_send.at[r],
                        part_recv.at[r],
                        {"expert": j},
                    )

                @pl.when(j == me)
                def _():
                    pltpu.make_async_copy(
                        summed.at[r, at, cols], incoming.at[r, me], part_recv.at[r]
                    ).start()

    send_state(2, 1)

    holds = [[owner_slot[old_place[r, e]] for e in range(n)] for r in range(2)]

    def sum_of(r, k):
        total = None
        for e in range(n):
            weight = jnp.where(holds[r][e] == k, 1.0, 0.0).astype(F32)
            term = weight * incoming[r, e].astype(F32)
            total = term if total is None else total + term
        return total

    wait_bytes(incoming.at[0], part_recv.at[0])

    @pl.loop(0, n)
    def _(k):
        acc[k] = sum_of(0, k)

    wait_bytes(incoming.at[1], part_recv.at[1])

    @pl.loop(0, n)
    def _(d):
        k = lax.rem(me + d + 1, n)
        acc[k] = acc[k] + sum_of(1, k)
        to_owner[k] = acc[k].astype(BF16)

        @pl.when(k != me)
        def _():
            send(
                to_owner.at[k],
                slot_grad.at[my_rows, my_cols],
                owner_sem.at[0],
                owner_sem.at[1],
                {"expert": k},
            )

        @pl.when(k == me)
        def _():
            pltpu.make_async_copy(
                to_owner.at[k], slot_grad.at[my_rows, my_cols], owner_sem.at[1]
            ).start()

    wait_bytes(pieces_in.at[:, pl.ds(0, 2)], state_recv.at[0])
    wait_bytes(pieces_in.at[:, pl.ds(2, 1)], state_recv.at[2])

    @pl.loop(0, n)
    def _(k):
        fresh[k] = adam(
            pieces_in[k, 0].astype(F32),
            pieces_in[k, 1].astype(F32),
            pieces_in[k, 2].astype(F32),
            acc[k],
        )[0].astype(BF16)

    for d in range(1, n + 1):
        j = lax.rem(me + d, n)
        for r in range(2):
            outbound[j, r] = fresh[owner_slot[new_place[r, j]]]
        there = replicas.at[:, my_rows, my_cols]
        if d < n:
            send(outbound.at[j], there, fresh_sem.at[0], fresh_sem.at[1], {"expert": j})
        else:
            pltpu.make_async_copy(outbound.at[j], there, fresh_sem.at[1]).start()

    wait_bytes(slot_grad, owner_sem.at[1])

    @pl.loop(0, n)
    def _(e):
        rows, cols = piece_at(e, width)
        result = adam(
            state[0, rows, cols],
            state[1, rows, cols],
            state[2, rows, cols],
            slot_grad[rows, cols].astype(F32),
        )
        for i, out in enumerate((new_master, new_moment, new_second)):
            out[0, rows, cols] = result[i]

    others = pl.ds(0, n - 1)
    wait_bytes(own, core_send)
    wait_bytes(cross_out, cross_send)
    wait_bytes(pieces_in.at[others, pl.ds(0, 2)], state_send.at[0])
    wait_bytes(pieces_in.at[others, pl.ds(2, 1)], state_send.at[2])
    for r in range(2):
        wait_bytes(incoming.at[r, others], part_send.at[r])
    wait_bytes(to_owner.at[others], owner_sem.at[0])
    wait_bytes(outbound.at[others], fresh_sem.at[0])
    wait_bytes(replicas, fresh_sem.at[1])


def hand_over(*refs):
    count = len(refs) // 2
    copies = [
        pltpu.make_async_copy(refs[i], refs[count + i], refs[-1].at[i]) for i in range(count)
    ]
    for copy in copies:
        copy.start()
    for copy in copies:
        copy.wait()


def by_kernel(grads, master, moment, second, old_place, new_place, owner_slot):
    n = lax.axis_size("expert")
    quarter, cols = master.shape[1:]
    width = cols * 2 // n
    dma = pltpu.SemaphoreType.DMA
    any_spec = pl.BlockSpec(memory_space=pl.ANY)
    smem_spec = pl.BlockSpec(memory_space=pltpu.SMEM)
    out_shape = (jax.ShapeDtypeStruct(master.shape, F32),) * 3 + (
        jax.ShapeDtypeStruct((2, quarter, cols), BF16),
    )
    vmem_spec = pl.BlockSpec(memory_space=pltpu.VMEM)
    results = pl.pallas_call(
        functools.partial(kernel, n),
        out_shape=tuple(pltpu.VMEM(out.shape, out.dtype) for out in out_shape),
        in_specs=[any_spec] * 4 + [smem_spec] * 3,
        out_specs=(vmem_spec,) * 4,
        scratch_shapes=[
            pltpu.VMEM((2, 2, quarter, cols), BF16),
            pltpu.VMEM((2, 2, quarter, cols), BF16),
            pltpu.VMEM((2, quarter, cols), BF16),
            pltpu.VMEM((2, quarter, cols), BF16),
            pltpu.VMEM((2, quarter, cols), BF16),
            pltpu.VMEM((2, n, TILE, width), BF16),
            pltpu.VMEM((n, TILE, width), F32),
            pltpu.VMEM((n, TILE, width), BF16),
            pltpu.VMEM((quarter, cols), BF16),
            pltpu.VMEM((3, quarter, cols), F32),
            pltpu.VMEM((3, quarter, cols), BF16),
            pltpu.VMEM((n, 3, TILE, width), BF16),
            pltpu.VMEM((n, TILE, width), BF16),
            pltpu.VMEM((n, 2, TILE, width), BF16),
            dma((5,)),
            dma,
            dma((2, 4)),
            dma,
            dma((4,)),
            dma((2,)),
            dma((2,)),
            dma((3,)),
            dma((3,)),
            dma((2,)),
            dma((2,)),
        ],
        compiler_params=pltpu.CompilerParams(collective_id=0, has_side_effects=True),
        name="reduce_update_refresh",
    )(grads, master, moment, second, old_place.T, new_place.T, owner_slot)
    return pl.pallas_call(
        hand_over,
        out_shape=out_shape,
        in_specs=[vmem_spec] * 4,
        out_specs=(any_spec,) * 4,
        scratch_shapes=[dma((4,))],
        name="hand_over",
    )(*results)


def by_collectives(grads, master, moment, second, old_place, new_place, owner_slot):
    device_count = lax.axis_size("expert")
    slot_count = grads.shape[1]
    col_count = grads.shape[3]
    own_count = master.shape[0]
    quarter_rows = master.shape[1]
    piece_size = quarter_rows * col_count // device_count
    expert_count = owner_slot.shape[0]
    expert_ids = jnp.arange(expert_count, dtype=jnp.int32)
    old_hot = (expert_ids[:, None] == old_place.T.reshape(-1)[None, :]).astype(jnp.float32)
    summed = lax.psum_scatter(
        grads[0].astype(jnp.float32).astype(jnp.bfloat16), "dp", scatter_dimension=1, tiled=True
    ).astype(jnp.float32)
    incoming = lax.all_to_all(
        summed.reshape(slot_count, device_count, piece_size),
        "expert",
        split_axis=1,
        concat_axis=1,
        tiled=True,
    )
    expert_part = jnp.dot(
        old_hot,
        incoming.reshape(slot_count * device_count, piece_size),
        precision=lax.Precision.HIGHEST,
    )
    slot_ids = jnp.arange(device_count * own_count, dtype=jnp.int32)
    owner_hot = (
        (slot_ids[:, None] == owner_slot[None, :])
        .astype(jnp.float32)
        .reshape(device_count, own_count, expert_count)
    )
    outgoing = jnp.einsum("koe,ep->okp", owner_hot, expert_part, precision=lax.Precision.HIGHEST)
    slot_grad = lax.all_to_all(outgoing, "expert", split_axis=1, concat_axis=1, tiled=True).reshape(
        own_count, quarter_rows, col_count
    )
    new_master, new_moment, new_second = adam(master, moment, second, slot_grad)
    fresh = new_master.astype(jnp.bfloat16).reshape(own_count, device_count, piece_size)
    every_slot = lax.all_to_all(fresh, "expert", split_axis=1, concat_axis=0, tiled=True).reshape(
        device_count * own_count, piece_size
    )
    wanted = owner_slot[new_place.T.reshape(-1)]
    outbound = jnp.take(every_slot, wanted, axis=0).reshape(slot_count, device_count, piece_size)
    received = lax.all_to_all(outbound, "expert", split_axis=1, concat_axis=1, tiled=True)
    replicas = received.reshape(slot_count, quarter_rows, col_count)
    return (new_master, new_moment, new_second, replicas)


def on_device(grads, master, moment, second, old_place, new_place, owner_slot):
    fits = (
        lax.axis_size("dp") == 4
        and lax.axis_size("expert") == 8
        and grads.shape[1] == 2
        and master.shape[0] == 1
        and owner_slot.shape[0] == 8
        and master.shape[1] == 2 * TILE
        and grads.shape[3] % (4 * 128) == 0
    )
    plan = by_kernel if fits else by_collectives
    return plan(grads, master, moment, second, old_place, new_place, owner_slot)


def solution(mesh):
    placed = (
        P("dp", "expert", None, None),
        P("expert", "dp", None),
        P("expert", "dp", None),
        P("expert", "dp", None),
        P(),
        P(),
        P(),
    )
    return jax.shard_map(
        on_device,
        mesh=mesh,
        in_specs=placed,
        out_specs=(
            P("expert", "dp", None),
            P("expert", "dp", None),
            P("expert", "dp", None),
            P("expert", "dp", None),
        ),
        check_vma=False,
    )
```

```python
import functools

import jax
import jax.numpy as jnp
from jax import lax
from jax.experimental import pallas as pl
from jax.experimental.pallas import tpu as pltpu
from jax.sharding import PartitionSpec as P

beta_first = 0.9
beta_second = 0.999
learn_rate = 0.02
weight_decay = 0.1
epsilon = 1e-08
scale_first = 1.0 - 0.9**40
scale_second = 1.0 - 0.999**40
MESH = pl.DeviceIdType.MESH
F32 = jnp.float32
BF16 = jnp.bfloat16
TILE = 16


def adam(master, moment, second, grad):
    new_moment = beta_first * moment + (1.0 - beta_first) * grad
    new_second = beta_second * second + (1.0 - beta_second) * grad * grad
    update = new_moment / scale_first / (jnp.sqrt(new_second / scale_second) + epsilon)
    new_master = master - learn_rate * (update + weight_decay * master)
    return new_master, new_moment, new_second


def piece_at(j, width):
    rows = pl.ds(pl.multiple_of(((j // 2) % 2) * TILE, TILE), TILE)
    cols = pl.ds(pl.multiple_of(((j // 4) * 2 + j % 2) * width, 128), width)
    return rows, cols


def kernel(
    n,
    grads,
    master,
    moment,
    second,
    old_place,
    new_place,
    owner_slot,
    new_master,
    new_moment,
    new_second,
    replicas,
    own,
    core_in,
    cross_out,
    cross_in,
    summed,
    incoming,
    acc,
    to_owner,
    slot_grad,
    state,
    state_out,
    pieces_in,
    fresh,
    outbound,
    load_sem,
    core_send,
    core_recv,
    cross_send,
    cross_recv,
    part_send,
    part_recv,
    state_send,
    state_recv,
    owner_sem,
    fresh_sem,
):
    me = lax.axis_index("expert")
    dp = lax.axis_index("dp")
    x, core = dp // 2, dp % 2
    near = x * 2 + (1 - core)
    far = (1 - x) * 2 + core
    quarter = master.shape[1]
    width = grads.shape[3] * 2 // n
    chunks = [(r, a) for r in range(2) for a in range(2)]

    def rows_of(dp_at, a=0, size=quarter):
        return pl.ds(pl.multiple_of(dp_at * quarter + a * TILE, TILE), size)

    def wait_bytes(ref, sem):
        pltpu.make_async_copy(ref, ref, sem).wait()

    def send(src, dst, send_sem, recv_sem, to):
        pltpu.make_async_remote_copy(
            src_ref=src,
            dst_ref=dst,
            send_sem=send_sem,
            recv_sem=recv_sem,
            device_id=to,
            device_id_type=MESH,
        ).start()

    loads = [
        pltpu.make_async_copy(src.at[0], state.at[i], load_sem.at[i])
        for i, src in enumerate((master, moment, second))
    ]
    loads += [
        pltpu.make_async_copy(
            grads.at[0, :, rows_of((1 - x) * 2 + core)], own.at[0], load_sem.at[3]
        ),
        pltpu.make_async_copy(grads.at[0, :, rows_of(dp)], own.at[1], load_sem.at[4]),
    ]
    barrier = pltpu.get_barrier_semaphore()
    for d in range(1, n):
        pl.semaphore_signal(
            barrier, inc=1, device_id={"expert": lax.rem(me + d, n)}, device_id_type=MESH
        )
    for other in (near, far):
        pl.semaphore_signal(barrier, inc=1, device_id={"dp": other}, device_id_type=MESH)
    for load in loads:
        load.start()
    for i in range(3):
        loads[i].wait()
        state_out[i] = state[i].astype(BF16)
    pl.semaphore_wait(barrier, n + 1)

    for half, x_at in ((0, 1 - x), (1, x)):
        for t, (r, a) in enumerate(chunks):
            send(
                grads.at[0, r, rows_of(x_at * 2 + (1 - core), a, TILE)],
                core_in.at[half, r, pl.ds(a * TILE, TILE)],
                core_send,
                core_recv.at[half, t],
                {"dp": near},
            )

    my_rows, my_cols = piece_at(me, width)

    def send_state(first, count):
        part = pl.ds(first, count)
        for d in range(1, n):
            j = lax.rem(me + d, n)
            rows, cols = piece_at(j, width)
            send(
                state_out.at[part, rows, cols],
                pieces_in.at[me, part],
                state_send.at[first],
                state_recv.at[first],
                {"expert": j},
            )
        pltpu.make_async_copy(
            state_out.at[part, my_rows, my_cols], pieces_in.at[me, part], state_recv.at[first]
        ).start()

    send_state(0, 2)

    loads[3].wait()
    for t, (r, a) in enumerate(chunks):
        at = pl.ds(a * TILE, TILE)
        wait_bytes(core_in.at[0, r, at], core_recv.at[0, t])
        cross_out[r, at] = (own[0, r, at].astype(F32) + core_in[0, r, at].astype(F32)).astype(BF16)
        send(cross_out.at[r, at], cross_in.at[r, at], cross_send, cross_recv.at[t], {"dp": far})

    loads[4].wait()
    for t, (r, a) in enumerate(chunks):
        at = pl.ds(a * TILE, TILE)
        wait_bytes(core_in.at[1, r, at], core_recv.at[1, t])
        wait_bytes(cross_in.at[r, at], cross_recv.at[t])
        summed[r, at] = (
            own[1, r, at].astype(F32)
            + core_in[1, r, at].astype(F32)
            + cross_in[r, at].astype(F32)
        ).astype(BF16)
        for high in range(2):
            for side in range(2):
                j = 4 * ((me // 4 + 1 + high) % 2) + 2 * a + (me % 2 + side) % 2
                rows, cols = piece_at(j, width)

                @pl.when(j != me)
                def _():
                    send(
                        summed.at[r, at, cols],
                        incoming.at[r, me],
                        part_send.at[r],
                        part_recv.at[r],
                        {"expert": j},
                    )

                @pl.when(j == me)
                def _():
                    pltpu.make_async_copy(
                        summed.at[r, at, cols], incoming.at[r, me], part_recv.at[r]
                    ).start()

    send_state(2, 1)

    holds = [[owner_slot[old_place[r, e]] for e in range(n)] for r in range(2)]

    def sum_of(r, k):
        total = None
        for e in range(n):
            weight = jnp.where(holds[r][e] == k, 1.0, 0.0).astype(F32)
            term = weight * incoming[r, e].astype(F32)
            total = term if total is None else total + term
        return total

    wait_bytes(incoming.at[0], part_recv.at[0])

    @pl.loop(0, n)
    def _(k):
        acc[k] = sum_of(0, k)

    wait_bytes(incoming.at[1], part_recv.at[1])

    @pl.loop(0, n)
    def _(d):
        k = lax.rem(me + d + 1, n)
        acc[k] = acc[k] + sum_of(1, k)
        to_owner[k] = acc[k].astype(BF16)

        @pl.when(k != me)
        def _():
            send(
                to_owner.at[k],
                slot_grad.at[my_rows, my_cols],
                owner_sem.at[0],
                owner_sem.at[1],
                {"expert": k},
            )

        @pl.when(k == me)
        def _():
            pltpu.make_async_copy(
                to_owner.at[k], slot_grad.at[my_rows, my_cols], owner_sem.at[1]
            ).start()

    wait_bytes(pieces_in.at[:, pl.ds(0, 2)], state_recv.at[0])
    wait_bytes(pieces_in.at[:, pl.ds(2, 1)], state_recv.at[2])

    @pl.loop(0, n)
    def _(k):
        fresh[k] = adam(
            pieces_in[k, 0].astype(F32),
            pieces_in[k, 1].astype(F32),
            pieces_in[k, 2].astype(F32),
            acc[k],
        )[0].astype(BF16)

    for d in range(1, n + 1):
        j = lax.rem(me + d, n)
        for r in range(2):
            outbound[j, r] = fresh[owner_slot[new_place[r, j]]]
        there = replicas.at[:, my_rows, my_cols]
        if d < n:
            send(outbound.at[j], there, fresh_sem.at[0], fresh_sem.at[1], {"expert": j})
        else:
            pltpu.make_async_copy(outbound.at[j], there, fresh_sem.at[1]).start()

    wait_bytes(slot_grad, owner_sem.at[1])

    @pl.loop(0, n)
    def _(e):
        rows, cols = piece_at(e, width)
        result = adam(
            state[0, rows, cols],
            state[1, rows, cols],
            state[2, rows, cols],
            slot_grad[rows, cols].astype(F32),
        )
        for i, out in enumerate((new_master, new_moment, new_second)):
            out[0, rows, cols] = result[i]

    others = pl.ds(0, n - 1)
    wait_bytes(own, core_send)
    wait_bytes(cross_out, cross_send)
    wait_bytes(pieces_in.at[others, pl.ds(0, 2)], state_send.at[0])
    wait_bytes(pieces_in.at[others, pl.ds(2, 1)], state_send.at[2])
    for r in range(2):
        wait_bytes(incoming.at[r, others], part_send.at[r])
    wait_bytes(to_owner.at[others], owner_sem.at[0])
    wait_bytes(outbound.at[others], fresh_sem.at[0])
    wait_bytes(replicas, fresh_sem.at[1])


def hand_over(*refs):
    count = len(refs) // 2
    copies = [
        pltpu.make_async_copy(refs[i], refs[count + i], refs[-1].at[i]) for i in range(count)
    ]
    for copy in copies:
        copy.start()
    for copy in copies:
        copy.wait()


def by_kernel(grads, master, moment, second, old_place, new_place, owner_slot):
    n = lax.axis_size("expert")
    quarter, cols = master.shape[1:]
    width = cols * 2 // n
    dma = pltpu.SemaphoreType.DMA
    any_spec = pl.BlockSpec(memory_space=pl.ANY)
    smem_spec = pl.BlockSpec(memory_space=pltpu.SMEM)
    out_shape = (jax.ShapeDtypeStruct(master.shape, F32),) * 3 + (
        jax.ShapeDtypeStruct((2, quarter, cols), BF16),
    )
    vmem_spec = pl.BlockSpec(memory_space=pltpu.VMEM)
    results = pl.pallas_call(
        functools.partial(kernel, n),
        out_shape=tuple(pltpu.VMEM(out.shape, out.dtype) for out in out_shape),
        in_specs=[any_spec] * 4 + [smem_spec] * 3,
        out_specs=(vmem_spec,) * 4,
        scratch_shapes=[
            pltpu.VMEM((2, 2, quarter, cols), BF16),
            pltpu.VMEM((2, 2, quarter, cols), BF16),
            pltpu.VMEM((2, quarter, cols), BF16),
            pltpu.VMEM((2, quarter, cols), BF16),
            pltpu.VMEM((2, quarter, cols), BF16),
            pltpu.VMEM((2, n, TILE, width), BF16),
            pltpu.VMEM((n, TILE, width), F32),
            pltpu.VMEM((n, TILE, width), BF16),
            pltpu.VMEM((quarter, cols), BF16),
            pltpu.VMEM((3, quarter, cols), F32),
            pltpu.VMEM((3, quarter, cols), BF16),
            pltpu.VMEM((n, 3, TILE, width), BF16),
            pltpu.VMEM((n, TILE, width), BF16),
            pltpu.VMEM((n, 2, TILE, width), BF16),
            dma((5,)),
            dma,
            dma((2, 4)),
            dma,
            dma((4,)),
            dma((2,)),
            dma((2,)),
            dma((3,)),
            dma((3,)),
            dma((2,)),
            dma((2,)),
        ],
        compiler_params=pltpu.CompilerParams(collective_id=0, has_side_effects=True),
        name="reduce_update_refresh",
    )(grads, master, moment, second, old_place.T, new_place.T, owner_slot)
    return pl.pallas_call(
        hand_over,
        out_shape=out_shape,
        in_specs=[any_spec] * 4,
        out_specs=(any_spec,) * 4,
        scratch_shapes=[dma((4,))],
        compiler_params=pltpu.CompilerParams(vmem_limit_bytes=1 << 20),
        name="hand_over",
    )(*[pltpu.with_memory_space_constraint(result, pltpu.VMEM) for result in results])


def by_collectives(grads, master, moment, second, old_place, new_place, owner_slot):
    device_count = lax.axis_size("expert")
    slot_count = grads.shape[1]
    col_count = grads.shape[3]
    own_count = master.shape[0]
    quarter_rows = master.shape[1]
    piece_size = quarter_rows * col_count // device_count
    expert_count = owner_slot.shape[0]
    expert_ids = jnp.arange(expert_count, dtype=jnp.int32)
    old_hot = (expert_ids[:, None] == old_place.T.reshape(-1)[None, :]).astype(jnp.float32)
    summed = lax.psum_scatter(
        grads[0].astype(jnp.float32).astype(jnp.bfloat16), "dp", scatter_dimension=1, tiled=True
    ).astype(jnp.float32)
    incoming = lax.all_to_all(
        summed.reshape(slot_count, device_count, piece_size),
        "expert",
        split_axis=1,
        concat_axis=1,
        tiled=True,
    )
    expert_part = jnp.dot(
        old_hot,
        incoming.reshape(slot_count * device_count, piece_size),
        precision=lax.Precision.HIGHEST,
    )
    slot_ids = jnp.arange(device_count * own_count, dtype=jnp.int32)
    owner_hot = (
        (slot_ids[:, None] == owner_slot[None, :])
        .astype(jnp.float32)
        .reshape(device_count, own_count, expert_count)
    )
    outgoing = jnp.einsum("koe,ep->okp", owner_hot, expert_part, precision=lax.Precision.HIGHEST)
    slot_grad = lax.all_to_all(outgoing, "expert", split_axis=1, concat_axis=1, tiled=True).reshape(
        own_count, quarter_rows, col_count
    )
    new_master, new_moment, new_second = adam(master, moment, second, slot_grad)
    fresh = new_master.astype(jnp.bfloat16).reshape(own_count, device_count, piece_size)
    every_slot = lax.all_to_all(fresh, "expert", split_axis=1, concat_axis=0, tiled=True).reshape(
        device_count * own_count, piece_size
    )
    wanted = owner_slot[new_place.T.reshape(-1)]
    outbound = jnp.take(every_slot, wanted, axis=0).reshape(slot_count, device_count, piece_size)
    received = lax.all_to_all(outbound, "expert", split_axis=1, concat_axis=1, tiled=True)
    replicas = received.reshape(slot_count, quarter_rows, col_count)
    return (new_master, new_moment, new_second, replicas)


def on_device(grads, master, moment, second, old_place, new_place, owner_slot):
    fits = (
        lax.axis_size("dp") == 4
        and lax.axis_size("expert") == 8
        and grads.shape[1] == 2
        and master.shape[0] == 1
        and owner_slot.shape[0] == 8
        and master.shape[1] == 2 * TILE
        and grads.shape[3] % (4 * 128) == 0
    )
    plan = by_kernel if fits else by_collectives
    return plan(grads, master, moment, second, old_place, new_place, owner_slot)


def solution(mesh):
    placed = (
        P("dp", "expert", None, None),
        P("expert", "dp", None),
        P("expert", "dp", None),
        P("expert", "dp", None),
        P(),
        P(),
        P(),
    )
    return jax.shard_map(
        on_device,
        mesh=mesh,
        in_specs=placed,
        out_specs=(
            P("expert", "dp", None),
            P("expert", "dp", None),
            P("expert", "dp", None),
            P("expert", "dp", None),
        ),
        check_vma=False,
    )
```

```python
import functools

import jax
import jax.numpy as jnp
from jax import lax
from jax.experimental import pallas as pl
from jax.experimental.pallas import tpu as pltpu
from jax.sharding import PartitionSpec as P

beta_first = 0.9
beta_second = 0.999
learn_rate = 0.02
weight_decay = 0.1
epsilon = 1e-08
scale_first = 1.0 - 0.9**40
scale_second = 1.0 - 0.999**40
MESH = pl.DeviceIdType.MESH
F32 = jnp.float32
BF16 = jnp.bfloat16
TILE = 16
LANES = 128


def adam(master, moment, second, grad):
    new_moment = beta_first * moment + (1.0 - beta_first) * grad
    new_second = beta_second * second + (1.0 - beta_second) * grad * grad
    update = new_moment / scale_first / (jnp.sqrt(new_second / scale_second) + epsilon)
    new_master = master - learn_rate * (update + weight_decay * master)
    return new_master, new_moment, new_second


def piece_at(j, n, cols, c):
    rows = pl.ds(pl.multiple_of(((j // 2) % 2) * TILE, TILE), TILE)
    start = c * (n // 2 * LANES) + ((j // 4) * 2 + j % 2) * LANES
    return rows, pl.ds(pl.multiple_of(start, LANES), LANES)


def kernel(
    n,
    grads,
    master,
    moment,
    second,
    old_place,
    new_place,
    owner_slot,
    new_master,
    new_moment,
    new_second,
    replicas,
    own,
    core_in,
    cross_out,
    cross_in,
    summed,
    incoming,
    to_owner,
    slot_grad,
    state,
    state_out,
    pieces_in,
    fresh,
    outbound,
    load_sem,
    core_send,
    core_recv,
    cross_send,
    cross_recv,
    part_send,
    part_recv,
    state_send,
    state_recv,
    owner_sem,
    fresh_sem,
):
    me = lax.axis_index("expert")
    dp = lax.axis_index("dp")
    x, core = dp // 2, dp % 2
    near = x * 2 + (1 - core)
    far = (1 - x) * 2 + core
    quarter = master.shape[1]
    width = grads.shape[3]
    span = n // 2 * LANES
    chunks = width // span

    def rows_of(dp_at):
        return pl.ds(pl.multiple_of(dp_at * quarter, TILE), quarter)

    def wait_bytes(ref, sem):
        pltpu.make_async_copy(ref, ref, sem).wait()

    def send(src, dst, send_sem, recv_sem, to):
        pltpu.make_async_remote_copy(
            src_ref=src,
            dst_ref=dst,
            send_sem=send_sem,
            recv_sem=recv_sem,
            device_id=to,
            device_id_type=MESH,
        ).start()

    loads = [
        pltpu.make_async_copy(src.at[0], state.at[i], load_sem.at[i])
        for i, src in enumerate((master, moment, second))
    ]
    loads += [
        pltpu.make_async_copy(
            grads.at[0, :, rows_of((1 - x) * 2 + core)], own.at[0], load_sem.at[3]
        ),
        pltpu.make_async_copy(grads.at[0, :, rows_of(dp)], own.at[1], load_sem.at[4]),
    ]
    barrier = pltpu.get_barrier_semaphore()
    for d in range(1, n):
        pl.semaphore_signal(
            barrier, inc=1, device_id={"expert": lax.rem(me + d, n)}, device_id_type=MESH
        )
    for other in (near, far):
        pl.semaphore_signal(barrier, inc=1, device_id={"dp": other}, device_id_type=MESH)
    for load in loads:
        load.start()
    for i in range(3):
        loads[i].wait()
        for j in range(n):
            for c in range(chunks):
                rows, cols = piece_at(j, n, width, c)
                state_out[j, i, :, c * LANES : (c + 1) * LANES] = state[i, rows, cols].astype(BF16)
    pl.semaphore_wait(barrier, n + 1)

    for half, x_at in ((0, 1 - x), (1, x)):
        for c in range(chunks):
            at = pl.ds(c * span, span)
            send(
                grads.at[0, :, rows_of(x_at * 2 + (1 - core)), at],
                core_in.at[half, :, :, at],
                core_send,
                core_recv.at[half, c],
                {"dp": near},
            )

    for d in range(1, n):
        j = lax.rem(me + d, n)
        send(state_out.at[j], pieces_in.at[me], state_send, state_recv, {"expert": j})
    pltpu.make_async_copy(state_out.at[me], pieces_in.at[me], state_recv).start()

    loads[3].wait()
    for c in range(chunks):
        at = pl.ds(c * span, span)
        wait_bytes(core_in.at[0, :, :, at], core_recv.at[0, c])
        cross_out[:, :, at] = (
            own[0, :, :, at].astype(F32) + core_in[0, :, :, at].astype(F32)
        ).astype(BF16)
        send(
            cross_out.at[:, :, at],
            cross_in.at[:, :, at],
            cross_send,
            cross_recv.at[c],
            {"dp": far},
        )
    loads[4].wait()

    def exchange(c):
        at = pl.ds(c * span, span)
        wait_bytes(core_in.at[1, :, :, at], core_recv.at[1, c])
        wait_bytes(cross_in.at[:, :, at], cross_recv.at[c])
        summed[:, :, at] = (
            own[1, :, :, at].astype(F32)
            + core_in[1, :, :, at].astype(F32)
            + cross_in[:, :, at].astype(F32)
        ).astype(BF16)
        for d in range(1, n + 1):
            j = lax.rem(me + d, n)
            rows, cols = piece_at(j, n, width, c)
            src, dst = summed.at[:, rows, cols], incoming.at[c, me]
            if d < n:
                send(src, dst, part_send, part_recv.at[c], {"expert": j})
            else:
                pltpu.make_async_copy(src, dst, part_recv.at[c]).start()

    holds = [[owner_slot[old_place[r, e]] for e in range(n)] for r in range(2)]

    def update(c):
        my_rows, my_cols = piece_at(me, n, width, c)
        lanes = pl.ds(c * LANES, LANES)
        wait_bytes(incoming.at[c], part_recv.at[c])
        if c == 0:
            wait_bytes(pieces_in, state_recv)

        @pl.loop(0, n)
        def _(d):
            k = lax.rem(me + d + 1, n)
            total = None
            for r in range(2):
                for e in range(n):
                    weight = jnp.where(holds[r][e] == k, 1.0, 0.0).astype(F32)
                    term = weight * incoming[c, e, r].astype(F32)
                    total = term if total is None else total + term
            to_owner[c, k] = total.astype(BF16)
            there = slot_grad.at[my_rows, my_cols]

            @pl.when(k != me)
            def _():
                send(to_owner.at[c, k], there, owner_sem.at[0], owner_sem.at[1], {"expert": k})

            @pl.when(k == me)
            def _():
                pltpu.make_async_copy(to_owner.at[c, k], there, owner_sem.at[1]).start()

            fresh[k] = adam(
                pieces_in[k, 0, :, lanes].astype(F32),
                pieces_in[k, 1, :, lanes].astype(F32),
                pieces_in[k, 2, :, lanes].astype(F32),
                total,
            )[0].astype(BF16)

        for d in range(1, n + 1):
            j = lax.rem(me + d, n)
            for r in range(2):
                outbound[c, j, r] = fresh[owner_slot[new_place[r, j]]]
            there = replicas.at[:, my_rows, my_cols]
            if d < n:
                send(outbound.at[c, j], there, fresh_sem.at[0], fresh_sem.at[1], {"expert": j})
            else:
                pltpu.make_async_copy(outbound.at[c, j], there, fresh_sem.at[1]).start()

    exchange(0)
    for c in range(1, chunks):
        exchange(c)
        update(c - 1)
    update(chunks - 1)

    wait_bytes(slot_grad, owner_sem.at[1])

    @pl.loop(0, n)
    def _(e):
        rows = pl.ds(pl.multiple_of((e % 2) * TILE, TILE), TILE)
        cols = pl.ds(pl.multiple_of((e // 2) * (2 * width // n), LANES), 2 * width // n)
        result = adam(
            state[0, rows, cols],
            state[1, rows, cols],
            state[2, rows, cols],
            slot_grad[rows, cols].astype(F32),
        )
        for i, out in enumerate((new_master, new_moment, new_second)):
            out[0, rows, cols] = result[i]

    others = pl.ds(0, n - 1)
    wait_bytes(own, core_send)
    wait_bytes(cross_out, cross_send)
    wait_bytes(pieces_in.at[others], state_send)
    wait_bytes(incoming.at[:, others], part_send)
    wait_bytes(to_owner.at[:, others], owner_sem.at[0])
    wait_bytes(outbound.at[:, others], fresh_sem.at[0])
    wait_bytes(replicas, fresh_sem.at[1])


def hand_over(*refs):
    count = len(refs) // 2
    copies = [
        pltpu.make_async_copy(refs[i], refs[count + i], refs[-1].at[i]) for i in range(count)
    ]
    for copy in copies:
        copy.start()
    for copy in copies:
        copy.wait()


def by_kernel(grads, master, moment, second, old_place, new_place, owner_slot):
    n = lax.axis_size("expert")
    quarter, cols = master.shape[1:]
    width = cols * 2 // n
    chunks = width // LANES
    dma = pltpu.SemaphoreType.DMA
    any_spec = pl.BlockSpec(memory_space=pl.ANY)
    smem_spec = pl.BlockSpec(memory_space=pltpu.SMEM)
    out_shape = (jax.ShapeDtypeStruct(master.shape, F32),) * 3 + (
        jax.ShapeDtypeStruct((2, quarter, cols), BF16),
    )
    vmem_spec = pl.BlockSpec(memory_space=pltpu.VMEM)
    results = pl.pallas_call(
        functools.partial(kernel, n),
        out_shape=tuple(pltpu.VMEM(out.shape, out.dtype) for out in out_shape),
        in_specs=[any_spec] * 4 + [smem_spec] * 3,
        out_specs=(vmem_spec,) * 4,
        scratch_shapes=[
            pltpu.VMEM((2, 2, quarter, cols), BF16),
            pltpu.VMEM((2, 2, quarter, cols), BF16),
            pltpu.VMEM((2, quarter, cols), BF16),
            pltpu.VMEM((2, quarter, cols), BF16),
            pltpu.VMEM((2, quarter, cols), BF16),
            pltpu.VMEM((chunks, n, 2, TILE, LANES), BF16),
            pltpu.VMEM((chunks, n, TILE, LANES), BF16),
            pltpu.VMEM((quarter, cols), BF16),
            pltpu.VMEM((3, quarter, cols), F32),
            pltpu.VMEM((n, 3, TILE, width), BF16),
            pltpu.VMEM((n, 3, TILE, width), BF16),
            pltpu.VMEM((n, TILE, LANES), BF16),
            pltpu.VMEM((chunks, n, 2, TILE, LANES), BF16),
            dma((5,)),
            dma,
            dma((2, chunks)),
            dma,
            dma((chunks,)),
            dma,
            dma((chunks,)),
            dma,
            dma,
            dma((2,)),
            dma((2,)),
        ],
        compiler_params=pltpu.CompilerParams(collective_id=0, has_side_effects=True),
        name="reduce_update_refresh",
    )(grads, master, moment, second, old_place.T, new_place.T, owner_slot)
    return pl.pallas_call(
        hand_over,
        out_shape=out_shape,
        in_specs=[any_spec] * 4,
        out_specs=(any_spec,) * 4,
        scratch_shapes=[dma((4,))],
        compiler_params=pltpu.CompilerParams(vmem_limit_bytes=1 << 20),
        name="hand_over",
    )(*[pltpu.with_memory_space_constraint(result, pltpu.VMEM) for result in results])


def by_collectives(grads, master, moment, second, old_place, new_place, owner_slot):
    device_count = lax.axis_size("expert")
    slot_count = grads.shape[1]
    col_count = grads.shape[3]
    own_count = master.shape[0]
    quarter_rows = master.shape[1]
    piece_size = quarter_rows * col_count // device_count
    expert_count = owner_slot.shape[0]
    expert_ids = jnp.arange(expert_count, dtype=jnp.int32)
    old_hot = (expert_ids[:, None] == old_place.T.reshape(-1)[None, :]).astype(jnp.float32)
    summed = lax.psum_scatter(
        grads[0].astype(jnp.float32).astype(jnp.bfloat16), "dp", scatter_dimension=1, tiled=True
    ).astype(jnp.float32)
    incoming = lax.all_to_all(
        summed.reshape(slot_count, device_count, piece_size),
        "expert",
        split_axis=1,
        concat_axis=1,
        tiled=True,
    )
    expert_part = jnp.dot(
        old_hot,
        incoming.reshape(slot_count * device_count, piece_size),
        precision=lax.Precision.HIGHEST,
    )
    slot_ids = jnp.arange(device_count * own_count, dtype=jnp.int32)
    owner_hot = (
        (slot_ids[:, None] == owner_slot[None, :])
        .astype(jnp.float32)
        .reshape(device_count, own_count, expert_count)
    )
    outgoing = jnp.einsum("koe,ep->okp", owner_hot, expert_part, precision=lax.Precision.HIGHEST)
    slot_grad = lax.all_to_all(outgoing, "expert", split_axis=1, concat_axis=1, tiled=True).reshape(
        own_count, quarter_rows, col_count
    )
    new_master, new_moment, new_second = adam(master, moment, second, slot_grad)
    fresh = new_master.astype(jnp.bfloat16).reshape(own_count, device_count, piece_size)
    every_slot = lax.all_to_all(fresh, "expert", split_axis=1, concat_axis=0, tiled=True).reshape(
        device_count * own_count, piece_size
    )
    wanted = owner_slot[new_place.T.reshape(-1)]
    outbound = jnp.take(every_slot, wanted, axis=0).reshape(slot_count, device_count, piece_size)
    received = lax.all_to_all(outbound, "expert", split_axis=1, concat_axis=1, tiled=True)
    replicas = received.reshape(slot_count, quarter_rows, col_count)
    return (new_master, new_moment, new_second, replicas)


def on_device(grads, master, moment, second, old_place, new_place, owner_slot):
    fits = (
        lax.axis_size("dp") == 4
        and lax.axis_size("expert") == 8
        and grads.shape[1] == 2
        and master.shape[0] == 1
        and owner_slot.shape[0] == 8
        and master.shape[1] == 2 * TILE
        and grads.shape[3] % (4 * 128) == 0
    )
    plan = by_kernel if fits else by_collectives
    return plan(grads, master, moment, second, old_place, new_place, owner_slot)


def solution(mesh):
    placed = (
        P("dp", "expert", None, None),
        P("expert", "dp", None),
        P("expert", "dp", None),
        P("expert", "dp", None),
        P(),
        P(),
        P(),
    )
    return jax.shard_map(
        on_device,
        mesh=mesh,
        in_specs=placed,
        out_specs=(
            P("expert", "dp", None),
            P("expert", "dp", None),
            P("expert", "dp", None),
            P("expert", "dp", None),
        ),
        check_vma=False,
    )
```

```python
import functools

import jax
import jax.numpy as jnp
from jax import lax
from jax.experimental import pallas as pl
from jax.experimental.pallas import tpu as pltpu
from jax.sharding import PartitionSpec as P

beta_first = 0.9
beta_second = 0.999
learn_rate = 0.02
weight_decay = 0.1
epsilon = 1e-08
scale_first = 1.0 - 0.9**40
scale_second = 1.0 - 0.999**40
MESH = pl.DeviceIdType.MESH
F32 = jnp.float32
BF16 = jnp.bfloat16
TILE = 16


def adam(master, moment, second, grad):
    new_moment = beta_first * moment + (1.0 - beta_first) * grad
    new_second = beta_second * second + (1.0 - beta_second) * grad * grad
    update = new_moment / scale_first / (jnp.sqrt(new_second / scale_second) + epsilon)
    new_master = master - learn_rate * (update + weight_decay * master)
    return new_master, new_moment, new_second


def piece_at(j, width):
    rows = pl.ds(pl.multiple_of(((j // 2) % 2) * TILE, TILE), TILE)
    cols = pl.ds(pl.multiple_of(((j // 4) * 2 + j % 2) * width, 128), width)
    return rows, cols


def kernel(
    n,
    grads,
    master,
    moment,
    second,
    old_place,
    new_place,
    owner_slot,
    new_master,
    new_moment,
    new_second,
    replicas,
    own,
    core_in,
    cross_out,
    cross_in,
    summed,
    incoming,
    acc,
    to_owner,
    slot_grad,
    state,
    state_out,
    pieces_in,
    fresh,
    outbound,
    load_sem,
    core_send,
    core_recv,
    cross_send,
    cross_recv,
    part_send,
    part_recv,
    state_send,
    state_recv,
    owner_sem,
    fresh_sem,
):
    me = lax.axis_index("expert")
    dp = lax.axis_index("dp")
    x, core = dp // 2, dp % 2
    near = x * 2 + (1 - core)
    far = (1 - x) * 2 + core
    quarter = master.shape[1]
    width = grads.shape[3] * 2 // n
    chunks = [(r, a) for r in range(2) for a in range(2)]

    def rows_of(dp_at, a=0, size=quarter):
        return pl.ds(pl.multiple_of(dp_at * quarter + a * TILE, TILE), size)

    def wait_bytes(ref, sem):
        pltpu.make_async_copy(ref, ref, sem).wait()

    def send(src, dst, send_sem, recv_sem, to):
        pltpu.make_async_remote_copy(
            src_ref=src,
            dst_ref=dst,
            send_sem=send_sem,
            recv_sem=recv_sem,
            device_id=to,
            device_id_type=MESH,
        ).start()

    loads = [
        pltpu.make_async_copy(src.at[0], state.at[i], load_sem.at[i])
        for i, src in enumerate((master, moment, second))
    ]
    loads += [
        pltpu.make_async_copy(
            grads.at[0, :, rows_of((1 - x) * 2 + core)], own.at[0], load_sem.at[3]
        ),
        pltpu.make_async_copy(grads.at[0, :, rows_of(dp)], own.at[1], load_sem.at[4]),
    ]
    barrier = pltpu.get_barrier_semaphore()
    for d in range(1, n):
        pl.semaphore_signal(
            barrier, inc=1, device_id={"expert": lax.rem(me + d, n)}, device_id_type=MESH
        )
    for other in (near, far):
        pl.semaphore_signal(barrier, inc=1, device_id={"dp": other}, device_id_type=MESH)
    for load in loads:
        load.start()
    for i in range(3):
        loads[i].wait()
        for j in range(n):
            rows, cols = piece_at(j, width)
            state_out[j, i] = state[i, rows, cols].astype(BF16)
    pl.semaphore_wait(barrier, n + 1)

    for half, x_at in ((0, 1 - x), (1, x)):
        for t, (r, a) in enumerate(chunks):
            send(
                grads.at[0, r, rows_of(x_at * 2 + (1 - core), a, TILE)],
                core_in.at[half, r, pl.ds(a * TILE, TILE)],
                core_send,
                core_recv.at[half, t],
                {"dp": near},
            )

    my_rows, my_cols = piece_at(me, width)

    for d in range(1, n):
        j = lax.rem(me + d, n)
        send(state_out.at[j], pieces_in.at[me], state_send, state_recv, {"expert": j})
    pltpu.make_async_copy(state_out.at[me], pieces_in.at[me], state_recv).start()

    loads[3].wait()
    for t, (r, a) in enumerate(chunks):
        at = pl.ds(a * TILE, TILE)
        wait_bytes(core_in.at[0, r, at], core_recv.at[0, t])
        cross_out[r, at] = (own[0, r, at].astype(F32) + core_in[0, r, at].astype(F32)).astype(BF16)
        send(cross_out.at[r, at], cross_in.at[r, at], cross_send, cross_recv.at[t], {"dp": far})

    loads[4].wait()
    for t, (r, a) in enumerate(chunks):
        at = pl.ds(a * TILE, TILE)
        wait_bytes(core_in.at[1, r, at], core_recv.at[1, t])
        wait_bytes(cross_in.at[r, at], cross_recv.at[t])
        total = (
            own[1, r, at].astype(F32)
            + core_in[1, r, at].astype(F32)
            + cross_in[r, at].astype(F32)
        ).astype(BF16)
        for j in range(2 * a, n, 4):
            for j_at in (j, j + 1):
                b = (j_at // 4) * 2 + j_at % 2
                summed[r, j_at] = total[:, b * width : (b + 1) * width]
        for high in range(2):
            for side in range(2):
                j = 4 * ((me // 4 + 1 + high) % 2) + 2 * a + (me % 2 + side) % 2

                @pl.when(j != me)
                def _():
                    send(
                        summed.at[r, j],
                        incoming.at[r, me],
                        part_send.at[r],
                        part_recv.at[r],
                        {"expert": j},
                    )

                @pl.when(j == me)
                def _():
                    pltpu.make_async_copy(
                        summed.at[r, j], incoming.at[r, me], part_recv.at[r]
                    ).start()

    holds = [[owner_slot[old_place[r, e]] for e in range(n)] for r in range(2)]

    def sum_of(r, k):
        total = None
        for e in range(n):
            weight = jnp.where(holds[r][e] == k, 1.0, 0.0).astype(F32)
            term = weight * incoming[r, e].astype(F32)
            total = term if total is None else total + term
        return total

    wait_bytes(incoming.at[0], part_recv.at[0])

    @pl.loop(0, n)
    def _(k):
        acc[k] = sum_of(0, k)

    wait_bytes(incoming.at[1], part_recv.at[1])

    @pl.loop(0, n)
    def _(d):
        k = lax.rem(me + d + 1, n)
        acc[k] = acc[k] + sum_of(1, k)
        to_owner[k] = acc[k].astype(BF16)

        @pl.when(k != me)
        def _():
            send(
                to_owner.at[k],
                slot_grad.at[me],
                owner_sem.at[0],
                owner_sem.at[1],
                {"expert": k},
            )

        @pl.when(k == me)
        def _():
            pltpu.make_async_copy(
                to_owner.at[k], slot_grad.at[me], owner_sem.at[1]
            ).start()

    wait_bytes(pieces_in, state_recv)

    @pl.loop(0, n)
    def _(k):
        fresh[k] = adam(
            pieces_in[k, 0].astype(F32),
            pieces_in[k, 1].astype(F32),
            pieces_in[k, 2].astype(F32),
            acc[k],
        )[0].astype(BF16)

    for d in range(1, n + 1):
        j = lax.rem(me + d, n)
        for r in range(2):
            outbound[j, r] = fresh[owner_slot[new_place[r, j]]]
        there = replicas.at[:, my_rows, my_cols]
        if d < n:
            send(outbound.at[j], there, fresh_sem.at[0], fresh_sem.at[1], {"expert": j})
        else:
            pltpu.make_async_copy(outbound.at[j], there, fresh_sem.at[1]).start()

    wait_bytes(slot_grad, owner_sem.at[1])

    @pl.loop(0, n)
    def _(e):
        rows, cols = piece_at(e, width)
        result = adam(
            state[0, rows, cols],
            state[1, rows, cols],
            state[2, rows, cols],
            slot_grad[e].astype(F32),
        )
        for i, out in enumerate((new_master, new_moment, new_second)):
            out[0, rows, cols] = result[i]

    others = pl.ds(0, n - 1)
    wait_bytes(own, core_send)
    wait_bytes(cross_out, cross_send)
    wait_bytes(pieces_in.at[others], state_send)
    for r in range(2):
        wait_bytes(incoming.at[r, others], part_send.at[r])
    wait_bytes(to_owner.at[others], owner_sem.at[0])
    wait_bytes(outbound.at[others], fresh_sem.at[0])
    wait_bytes(replicas, fresh_sem.at[1])


def hand_over(*refs):
    count = len(refs) // 2
    copies = [
        pltpu.make_async_copy(refs[i], refs[count + i], refs[-1].at[i]) for i in range(count)
    ]
    for copy in copies:
        copy.start()
    for copy in copies:
        copy.wait()


def by_kernel(grads, master, moment, second, old_place, new_place, owner_slot):
    n = lax.axis_size("expert")
    quarter, cols = master.shape[1:]
    width = cols * 2 // n
    dma = pltpu.SemaphoreType.DMA
    any_spec = pl.BlockSpec(memory_space=pl.ANY)
    smem_spec = pl.BlockSpec(memory_space=pltpu.SMEM)
    out_shape = (jax.ShapeDtypeStruct(master.shape, F32),) * 3 + (
        jax.ShapeDtypeStruct((2, quarter, cols), BF16),
    )
    vmem_spec = pl.BlockSpec(memory_space=pltpu.VMEM)
    results = pl.pallas_call(
        functools.partial(kernel, n),
        out_shape=tuple(pltpu.VMEM(out.shape, out.dtype) for out in out_shape),
        in_specs=[any_spec] * 4 + [smem_spec] * 3,
        out_specs=(vmem_spec,) * 4,
        scratch_shapes=[
            pltpu.VMEM((2, 2, quarter, cols), BF16),
            pltpu.VMEM((2, 2, quarter, cols), BF16),
            pltpu.VMEM((2, quarter, cols), BF16),
            pltpu.VMEM((2, quarter, cols), BF16),
            pltpu.VMEM((2, n, TILE, width), BF16),
            pltpu.VMEM((2, n, TILE, width), BF16),
            pltpu.VMEM((n, TILE, width), F32),
            pltpu.VMEM((n, TILE, width), BF16),
            pltpu.VMEM((n, TILE, width), BF16),
            pltpu.VMEM((3, quarter, cols), F32),
            pltpu.VMEM((n, 3, TILE, width), BF16),
            pltpu.VMEM((n, 3, TILE, width), BF16),
            pltpu.VMEM((n, TILE, width), BF16),
            pltpu.VMEM((n, 2, TILE, width), BF16),
            dma((5,)),
            dma,
            dma((2, 4)),
            dma,
            dma((4,)),
            dma((2,)),
            dma((2,)),
            dma,
            dma,
            dma((2,)),
            dma((2,)),
        ],
        compiler_params=pltpu.CompilerParams(collective_id=0, has_side_effects=True),
        name="reduce_update_refresh",
    )(grads, master, moment, second, old_place.T, new_place.T, owner_slot)
    return pl.pallas_call(
        hand_over,
        out_shape=out_shape,
        in_specs=[any_spec] * 4,
        out_specs=(any_spec,) * 4,
        scratch_shapes=[dma((4,))],
        compiler_params=pltpu.CompilerParams(vmem_limit_bytes=1 << 20),
        name="hand_over",
    )(*[pltpu.with_memory_space_constraint(result, pltpu.VMEM) for result in results])


def by_collectives(grads, master, moment, second, old_place, new_place, owner_slot):
    device_count = lax.axis_size("expert")
    slot_count = grads.shape[1]
    col_count = grads.shape[3]
    own_count = master.shape[0]
    quarter_rows = master.shape[1]
    piece_size = quarter_rows * col_count // device_count
    expert_count = owner_slot.shape[0]
    expert_ids = jnp.arange(expert_count, dtype=jnp.int32)
    old_hot = (expert_ids[:, None] == old_place.T.reshape(-1)[None, :]).astype(jnp.float32)
    summed = lax.psum_scatter(
        grads[0].astype(jnp.float32).astype(jnp.bfloat16), "dp", scatter_dimension=1, tiled=True
    ).astype(jnp.float32)
    incoming = lax.all_to_all(
        summed.reshape(slot_count, device_count, piece_size),
        "expert",
        split_axis=1,
        concat_axis=1,
        tiled=True,
    )
    expert_part = jnp.dot(
        old_hot,
        incoming.reshape(slot_count * device_count, piece_size),
        precision=lax.Precision.HIGHEST,
    )
    slot_ids = jnp.arange(device_count * own_count, dtype=jnp.int32)
    owner_hot = (
        (slot_ids[:, None] == owner_slot[None, :])
        .astype(jnp.float32)
        .reshape(device_count, own_count, expert_count)
    )
    outgoing = jnp.einsum("koe,ep->okp", owner_hot, expert_part, precision=lax.Precision.HIGHEST)
    slot_grad = lax.all_to_all(outgoing, "expert", split_axis=1, concat_axis=1, tiled=True).reshape(
        own_count, quarter_rows, col_count
    )
    new_master, new_moment, new_second = adam(master, moment, second, slot_grad)
    fresh = new_master.astype(jnp.bfloat16).reshape(own_count, device_count, piece_size)
    every_slot = lax.all_to_all(fresh, "expert", split_axis=1, concat_axis=0, tiled=True).reshape(
        device_count * own_count, piece_size
    )
    wanted = owner_slot[new_place.T.reshape(-1)]
    outbound = jnp.take(every_slot, wanted, axis=0).reshape(slot_count, device_count, piece_size)
    received = lax.all_to_all(outbound, "expert", split_axis=1, concat_axis=1, tiled=True)
    replicas = received.reshape(slot_count, quarter_rows, col_count)
    return (new_master, new_moment, new_second, replicas)


def on_device(grads, master, moment, second, old_place, new_place, owner_slot):
    fits = (
        lax.axis_size("dp") == 4
        and lax.axis_size("expert") == 8
        and grads.shape[1] == 2
        and master.shape[0] == 1
        and owner_slot.shape[0] == 8
        and master.shape[1] == 2 * TILE
        and grads.shape[3] % (4 * 128) == 0
    )
    plan = by_kernel if fits else by_collectives
    return plan(grads, master, moment, second, old_place, new_place, owner_slot)


def solution(mesh):
    placed = (
        P("dp", "expert", None, None),
        P("expert", "dp", None),
        P("expert", "dp", None),
        P("expert", "dp", None),
        P(),
        P(),
        P(),
    )
    return jax.shard_map(
        on_device,
        mesh=mesh,
        in_specs=placed,
        out_specs=(
            P("expert", "dp", None),
            P("expert", "dp", None),
            P("expert", "dp", None),
            P("expert", "dp", None),
        ),
        check_vma=False,
    )
```

```python
import functools

import jax
import jax.numpy as jnp
from jax import lax
from jax.experimental import pallas as pl
from jax.experimental.pallas import tpu as pltpu
from jax.sharding import PartitionSpec as P

beta_first = 0.9
beta_second = 0.999
learn_rate = 0.02
weight_decay = 0.1
epsilon = 1e-08
scale_first = 1.0 - 0.9**40
scale_second = 1.0 - 0.999**40
MESH = pl.DeviceIdType.MESH
F32 = jnp.float32
BF16 = jnp.bfloat16
TILE = 16


def adam(master, moment, second, grad):
    new_moment = beta_first * moment + (1.0 - beta_first) * grad
    new_second = beta_second * second + (1.0 - beta_second) * grad * grad
    update = new_moment / scale_first / (jnp.sqrt(new_second / scale_second) + epsilon)
    new_master = master - learn_rate * (update + weight_decay * master)
    return new_master, new_moment, new_second


def piece_at(j, width):
    rows = pl.ds(pl.multiple_of(((j // 2) % 2) * TILE, TILE), TILE)
    cols = pl.ds(pl.multiple_of(((j // 4) * 2 + j % 2) * width, 128), width)
    return rows, cols


def kernel(
    n,
    grads,
    master,
    moment,
    second,
    old_place,
    new_place,
    owner_slot,
    new_master,
    new_moment,
    new_second,
    replicas,
    own,
    core_in,
    cross_out,
    cross_in,
    summed,
    incoming,
    acc,
    to_owner,
    slot_grad,
    state,
    state_out,
    pieces_in,
    fresh,
    outbound,
    load_sem,
    core_send,
    core_recv,
    cross_send,
    cross_recv,
    part_send,
    part_recv,
    state_send,
    state_recv,
    owner_sem,
    fresh_sem,
):
    me = lax.axis_index("expert")
    dp = lax.axis_index("dp")
    x, core = dp // 2, dp % 2
    near = x * 2 + (1 - core)
    far = (1 - x) * 2 + core
    quarter = master.shape[1]
    width = grads.shape[3] * 2 // n
    chunks = [(r, a) for r in range(2) for a in range(2)]

    def rows_of(dp_at, a=0, size=quarter):
        return pl.ds(pl.multiple_of(dp_at * quarter + a * TILE, TILE), size)

    def wait_bytes(ref, sem):
        pltpu.make_async_copy(ref, ref, sem).wait()

    def send(src, dst, send_sem, recv_sem, to):
        pltpu.make_async_remote_copy(
            src_ref=src,
            dst_ref=dst,
            send_sem=send_sem,
            recv_sem=recv_sem,
            device_id=to,
            device_id_type=MESH,
        ).start()

    loads = [
        pltpu.make_async_copy(src.at[0], state.at[i], load_sem.at[i])
        for i, src in enumerate((master, moment, second))
    ]
    loads += [
        pltpu.make_async_copy(
            grads.at[0, :, rows_of((1 - x) * 2 + core)], own.at[0], load_sem.at[3]
        ),
        pltpu.make_async_copy(grads.at[0, :, rows_of(dp)], own.at[1], load_sem.at[4]),
    ]
    barrier = pltpu.get_barrier_semaphore()
    for d in range(1, n):
        pl.semaphore_signal(
            barrier, inc=1, device_id={"expert": lax.rem(me + d, n)}, device_id_type=MESH
        )
    for other in (near, far):
        pl.semaphore_signal(barrier, inc=1, device_id={"dp": other}, device_id_type=MESH)
    for load in loads:
        load.start()
    for i in range(3):
        loads[i].wait()
        for j in range(n):
            rows, cols = piece_at(j, width)
            state_out[j, i] = state[i, rows, cols].astype(BF16)
    pl.semaphore_wait(barrier, n + 1)

    for half, x_at in ((0, 1 - x), (1, x)):
        for t, (r, a) in enumerate(chunks):
            send(
                grads.at[0, r, rows_of(x_at * 2 + (1 - core), a, TILE)],
                core_in.at[half, r, pl.ds(a * TILE, TILE)],
                core_send,
                core_recv.at[half, t],
                {"dp": near},
            )

    my_rows, my_cols = piece_at(me, width)

    for d in range(1, n):
        j = lax.rem(me + d, n)
        send(state_out.at[j], pieces_in.at[me], state_send, state_recv, {"expert": j})
    pltpu.make_async_copy(state_out.at[me], pieces_in.at[me], state_recv).start()

    loads[3].wait()
    for t, (r, a) in enumerate(chunks):
        at = pl.ds(a * TILE, TILE)
        wait_bytes(core_in.at[0, r, at], core_recv.at[0, t])
        cross_out[r, at] = (own[0, r, at].astype(F32) + core_in[0, r, at].astype(F32)).astype(BF16)
        send(cross_out.at[r, at], cross_in.at[r, at], cross_send, cross_recv.at[t], {"dp": far})

    loads[4].wait()
    for t, (r, a) in enumerate(chunks):
        at = pl.ds(a * TILE, TILE)
        wait_bytes(core_in.at[1, r, at], core_recv.at[1, t])
        wait_bytes(cross_in.at[r, at], cross_recv.at[t])
        total = (
            own[1, r, at].astype(F32)
            + core_in[1, r, at].astype(F32)
            + cross_in[r, at].astype(F32)
        ).astype(BF16)
        for j in range(2 * a, n, 4):
            for j_at in (j, j + 1):
                b = (j_at // 4) * 2 + j_at % 2
                summed[r, j_at] = total[:, b * width : (b + 1) * width]
        for high in range(2):
            for side in range(2):
                j = 4 * ((me // 4 + 1 + high) % 2) + 2 * a + (me % 2 + side) % 2

                @pl.when(j != me)
                def _():
                    send(
                        summed.at[r, j],
                        incoming.at[r, me],
                        part_send.at[r],
                        part_recv.at[r],
                        {"expert": j},
                    )

                @pl.when(j == me)
                def _():
                    pltpu.make_async_copy(
                        summed.at[r, j], incoming.at[r, me], part_recv.at[r]
                    ).start()

    holds = [[owner_slot[old_place[r, e]] for e in range(n)] for r in range(2)]

    def sum_of(r, k):
        total = None
        for e in range(n):
            weight = jnp.where(holds[r][e] == k, 1.0, 0.0).astype(F32)
            term = weight * incoming[r, e].astype(F32)
            total = term if total is None else total + term
        return total

    wait_bytes(incoming.at[0], part_recv.at[0])

    @pl.loop(0, n)
    def _(k):
        acc[k] = sum_of(0, k)

    wait_bytes(pieces_in, state_recv)
    wait_bytes(incoming.at[1], part_recv.at[1])

    @pl.loop(0, n)
    def _(d):
        k = lax.rem(me + d + 1, n)
        total = acc[k] + sum_of(1, k)
        to_owner[k] = total.astype(BF16)

        @pl.when(k != me)
        def _():
            send(
                to_owner.at[k],
                slot_grad.at[me],
                owner_sem.at[0],
                owner_sem.at[1],
                {"expert": k},
            )

        @pl.when(k == me)
        def _():
            pltpu.make_async_copy(
                to_owner.at[k], slot_grad.at[me], owner_sem.at[1]
            ).start()

        fresh[k] = adam(
            pieces_in[k, 0].astype(F32),
            pieces_in[k, 1].astype(F32),
            pieces_in[k, 2].astype(F32),
            total,
        )[0].astype(BF16)

    for d in range(1, n + 1):
        j = lax.rem(me + d, n)
        for r in range(2):
            outbound[j, r] = fresh[owner_slot[new_place[r, j]]]
        there = replicas.at[:, my_rows, my_cols]
        if d < n:
            send(outbound.at[j], there, fresh_sem.at[0], fresh_sem.at[1], {"expert": j})
        else:
            pltpu.make_async_copy(outbound.at[j], there, fresh_sem.at[1]).start()

    wait_bytes(slot_grad, owner_sem.at[1])

    @pl.loop(0, n)
    def _(e):
        rows, cols = piece_at(e, width)
        result = adam(
            state[0, rows, cols],
            state[1, rows, cols],
            state[2, rows, cols],
            slot_grad[e].astype(F32),
        )
        for i, out in enumerate((new_master, new_moment, new_second)):
            out[0, rows, cols] = result[i]

    others = pl.ds(0, n - 1)
    wait_bytes(own, core_send)
    wait_bytes(cross_out, cross_send)
    wait_bytes(pieces_in.at[others], state_send)
    for r in range(2):
        wait_bytes(incoming.at[r, others], part_send.at[r])
    wait_bytes(to_owner.at[others], owner_sem.at[0])
    wait_bytes(outbound.at[others], fresh_sem.at[0])
    wait_bytes(replicas, fresh_sem.at[1])


def hand_over(*refs):
    count = len(refs) // 2
    copies = [
        pltpu.make_async_copy(refs[i], refs[count + i], refs[-1].at[i]) for i in range(count)
    ]
    for copy in copies:
        copy.start()
    for copy in copies:
        copy.wait()


def by_kernel(grads, master, moment, second, old_place, new_place, owner_slot):
    n = lax.axis_size("expert")
    quarter, cols = master.shape[1:]
    width = cols * 2 // n
    dma = pltpu.SemaphoreType.DMA
    any_spec = pl.BlockSpec(memory_space=pl.ANY)
    smem_spec = pl.BlockSpec(memory_space=pltpu.SMEM)
    out_shape = (jax.ShapeDtypeStruct(master.shape, F32),) * 3 + (
        jax.ShapeDtypeStruct((2, quarter, cols), BF16),
    )
    vmem_spec = pl.BlockSpec(memory_space=pltpu.VMEM)
    results = pl.pallas_call(
        functools.partial(kernel, n),
        out_shape=tuple(pltpu.VMEM(out.shape, out.dtype) for out in out_shape),
        in_specs=[any_spec] * 4 + [smem_spec] * 3,
        out_specs=(vmem_spec,) * 4,
        scratch_shapes=[
            pltpu.VMEM((2, 2, quarter, cols), BF16),
            pltpu.VMEM((2, 2, quarter, cols), BF16),
            pltpu.VMEM((2, quarter, cols), BF16),
            pltpu.VMEM((2, quarter, cols), BF16),
            pltpu.VMEM((2, n, TILE, width), BF16),
            pltpu.VMEM((2, n, TILE, width), BF16),
            pltpu.VMEM((n, TILE, width), F32),
            pltpu.VMEM((n, TILE, width), BF16),
            pltpu.VMEM((n, TILE, width), BF16),
            pltpu.VMEM((3, quarter, cols), F32),
            pltpu.VMEM((n, 3, TILE, width), BF16),
            pltpu.VMEM((n, 3, TILE, width), BF16),
            pltpu.VMEM((n, TILE, width), BF16),
            pltpu.VMEM((n, 2, TILE, width), BF16),
            dma((5,)),
            dma,
            dma((2, 4)),
            dma,
            dma((4,)),
            dma((2,)),
            dma((2,)),
            dma,
            dma,
            dma((2,)),
            dma((2,)),
        ],
        compiler_params=pltpu.CompilerParams(collective_id=0, has_side_effects=True),
        name="reduce_update_refresh",
    )(grads, master, moment, second, old_place.T, new_place.T, owner_slot)
    return pl.pallas_call(
        hand_over,
        out_shape=out_shape,
        in_specs=[any_spec] * 4,
        out_specs=(any_spec,) * 4,
        scratch_shapes=[dma((4,))],
        compiler_params=pltpu.CompilerParams(vmem_limit_bytes=1 << 20),
        name="hand_over",
    )(*[pltpu.with_memory_space_constraint(result, pltpu.VMEM) for result in results])


def by_collectives(grads, master, moment, second, old_place, new_place, owner_slot):
    device_count = lax.axis_size("expert")
    slot_count = grads.shape[1]
    col_count = grads.shape[3]
    own_count = master.shape[0]
    quarter_rows = master.shape[1]
    piece_size = quarter_rows * col_count // device_count
    expert_count = owner_slot.shape[0]
    expert_ids = jnp.arange(expert_count, dtype=jnp.int32)
    old_hot = (expert_ids[:, None] == old_place.T.reshape(-1)[None, :]).astype(jnp.float32)
    summed = lax.psum_scatter(
        grads[0].astype(jnp.float32).astype(jnp.bfloat16), "dp", scatter_dimension=1, tiled=True
    ).astype(jnp.float32)
    incoming = lax.all_to_all(
        summed.reshape(slot_count, device_count, piece_size),
        "expert",
        split_axis=1,
        concat_axis=1,
        tiled=True,
    )
    expert_part = jnp.dot(
        old_hot,
        incoming.reshape(slot_count * device_count, piece_size),
        precision=lax.Precision.HIGHEST,
    )
    slot_ids = jnp.arange(device_count * own_count, dtype=jnp.int32)
    owner_hot = (
        (slot_ids[:, None] == owner_slot[None, :])
        .astype(jnp.float32)
        .reshape(device_count, own_count, expert_count)
    )
    outgoing = jnp.einsum("koe,ep->okp", owner_hot, expert_part, precision=lax.Precision.HIGHEST)
    slot_grad = lax.all_to_all(outgoing, "expert", split_axis=1, concat_axis=1, tiled=True).reshape(
        own_count, quarter_rows, col_count
    )
    new_master, new_moment, new_second = adam(master, moment, second, slot_grad)
    fresh = new_master.astype(jnp.bfloat16).reshape(own_count, device_count, piece_size)
    every_slot = lax.all_to_all(fresh, "expert", split_axis=1, concat_axis=0, tiled=True).reshape(
        device_count * own_count, piece_size
    )
    wanted = owner_slot[new_place.T.reshape(-1)]
    outbound = jnp.take(every_slot, wanted, axis=0).reshape(slot_count, device_count, piece_size)
    received = lax.all_to_all(outbound, "expert", split_axis=1, concat_axis=1, tiled=True)
    replicas = received.reshape(slot_count, quarter_rows, col_count)
    return (new_master, new_moment, new_second, replicas)


def on_device(grads, master, moment, second, old_place, new_place, owner_slot):
    fits = (
        lax.axis_size("dp") == 4
        and lax.axis_size("expert") == 8
        and grads.shape[1] == 2
        and master.shape[0] == 1
        and owner_slot.shape[0] == 8
        and master.shape[1] == 2 * TILE
        and grads.shape[3] % (4 * 128) == 0
    )
    plan = by_kernel if fits else by_collectives
    return plan(grads, master, moment, second, old_place, new_place, owner_slot)


def solution(mesh):
    placed = (
        P("dp", "expert", None, None),
        P("expert", "dp", None),
        P("expert", "dp", None),
        P("expert", "dp", None),
        P(),
        P(),
        P(),
    )
    return jax.shard_map(
        on_device,
        mesh=mesh,
        in_specs=placed,
        out_specs=(
            P("expert", "dp", None),
            P("expert", "dp", None),
            P("expert", "dp", None),
            P("expert", "dp", None),
        ),
        check_vma=False,
    )
```
